512 devices in a mesh: ctx: 32 (over y, x_hi, core), head: 16 (over z, x_lo).
Axes of the slice: x: 4 (x_hi: 2, x_lo: 2; x = x_hi * 2 + x_lo), y: 8, z: 8, core: 2. Of those that a mesh axis runs over, the one named last changes fastest.
Arguments:
- queries: bfloat16 [8192, 4096], P('ctx', 'head'), may hold values from -13 to 13
- key_states: bfloat16 [8192, 2048], P('ctx', 'head'), may hold values from -12 to 12
- value_states: bfloat16 [8192, 2048], P('ctx', 'head'), may hold values from -6 to 6
- past_keys: bfloat16 [1024, 2048], P(None, 'head'), may hold values from -12 to 12
- past_values: bfloat16 [1024, 2048], P(None, 'head'), may hold values from -6 to 6
- out_weight: bfloat16 [4096, 5376], P('head'), may hold values from -0.125 to 0.125
Outputs:
- layer_output: bfloat16 [8192, 5376], P('ctx', 'head')
The draws below stay inside these ranges and needn't reach their ends.
All inputs are finite; a program needn't handle non-finite values.
Results may differ from the reference program's by a relative error of at most 0.025.
Values may be sent and summed in bfloat16 or wider, within the bound.
A program may use at most 64 MiB of HBM per device.

```python
import jax
import jax.numpy as jnp
from jax import lax

D = 5376
Q_HEADS = 32
KV_HEADS = 16
HEAD_DIM = 128
WINDOW = 1024
QUERY_SCALAR = 168
TOK_DEV = 256
TOKENS = 8192
REACH = 4
PAST = 1024
N_HEAD = 16


def draw_queries(key, part):
    key = jax.random.fold_in(key, 11)
    scale_key, entry_key = jax.random.split(key)
    row_scale = 10.0 ** jax.random.uniform(scale_key, (TOKENS, 1), jnp.float32, -0.5, 0.5)
    entries = jax.random.normal(entry_key, (TOKENS, Q_HEADS * HEAD_DIM), jnp.float32)
    entries = jnp.clip(entries * row_scale, -13.0, 13.0)
    return entries.astype(jnp.bfloat16)


def draw_key_states(key, part):
    key = jax.random.fold_in(key, 12)
    scale_key, entry_key = jax.random.split(key)
    row_scale = 1.5 * 10.0 ** jax.random.uniform(scale_key, (TOKENS, 1), jnp.float32, -0.5, 0.5)
    entries = jax.random.normal(entry_key, (TOKENS, KV_HEADS * HEAD_DIM), jnp.float32)
    entries = jnp.clip(entries * row_scale, -12.0, 12.0)
    return entries.astype(jnp.bfloat16)


def draw_past_keys(key, part):
    key = jax.random.fold_in(key, 13)
    scale_key, entry_key = jax.random.split(key)
    row_scale = 1.5 * 10.0 ** jax.random.uniform(scale_key, (PAST, 1), jnp.float32, -0.5, 0.5)
    entries = jax.random.normal(entry_key, (PAST, KV_HEADS * HEAD_DIM), jnp.float32)
    entries = jnp.clip(entries * row_scale, -12.0, 12.0)
    return entries.astype(jnp.bfloat16)


def with_spikes(result, stream_key, source, target, blocks, factor):
    def block_of(axis_at):
        return (jnp.arange(result.shape[axis_at]) // (result.shape[axis_at] // blocks)).reshape((-1,) + (1,) * (result.ndim - 1 - axis_at))

    first = jax.random.permutation(stream_key, blocks)[block_of(target)]
    far = (block_of(target) + blocks // 2) % blocks
    return jnp.where((block_of(source) == first) | (block_of(source) == far), factor * result, result)


def level_of(stream_key, dims, shards, least, largest):
    level = 1.0
    for position, parts in shards:
        steps = jax.random.uniform(jax.random.fold_in(jax.random.fold_in(stream_key, 6), position), (parts,), jnp.float32, least / len(shards), largest / len(shards))
        level = level * jnp.repeat(jnp.exp(steps), dims[position] // parts).reshape((-1,) + (1,) * (len(dims) - 1 - position))
    return level


def centred(rng, dims, spread, bound, shards=(), kind=jnp.bfloat16):
    array = spread * jax.random.normal(rng, dims, jnp.float32)
    if shards:
        array = array * level_of(rng, dims, shards, -0.22, 0.18)
    return jnp.clip(array, -bound, bound).astype(kind)


def noise_with(rng, shape, width, limit, cuts, heavy, kind=jnp.bfloat16):
    values = width * jax.random.normal(rng, shape, jnp.float32)
    if cuts:
        values = values * level_of(rng, shape, cuts, -0.22, 0.18)
    return jnp.clip(with_spikes(values, jax.random.fold_in(rng, 3), *heavy), -limit, limit).astype(kind)


def setup_inputs(seed: int = 0) -> dict:
    arg_keys = jax.random.split(jax.random.key(seed), 7)
    return {
        "queries": draw_queries(jax.random.fold_in(arg_keys[6], 71), 0),
        "key_states": draw_key_states(jax.random.fold_in(arg_keys[6], 71), 0),
        "value_states": centred(arg_keys[2], (TOKENS, KV_HEADS * HEAD_DIM), 1.0, 6.0, ((0, 32), (1, 16))),
        "past_keys": draw_past_keys(jax.random.fold_in(arg_keys[6], 71), 0),
        "past_values": centred(arg_keys[4], (PAST, KV_HEADS * HEAD_DIM), 1.0, 6.0, ((1, 16),)),
        "out_weight": noise_with(arg_keys[5], (Q_HEADS * HEAD_DIM, D), (Q_HEADS * HEAD_DIM) ** -0.5, 0.125, ((0, 16),), (0, 1, 16, 2.0)),
    }


def rounded(partial_term):
    return lax.optimization_barrier(partial_term.astype(jnp.bfloat16)).astype(jnp.float32)


def reference(queries, key_states, value_states, past_keys, past_values, out_weight):
    block_rows = TOK_DEV
    window_rows = (REACH + 1) * TOK_DEV
    group_size = Q_HEADS // KV_HEADS
    score_scale = QUERY_SCALAR ** -0.5
    every_key = jnp.concatenate([past_keys, key_states], axis=0)
    every_value = jnp.concatenate([past_values, value_states], axis=0)

    def attend(block_index):
        first_row = (block_index * block_rows).astype(jnp.int32)
        query_block = lax.dynamic_slice_in_dim(queries, first_row, block_rows, 0).astype(jnp.float32)
        query_block = query_block.reshape(block_rows, KV_HEADS, group_size, HEAD_DIM)
        key_block = lax.dynamic_slice_in_dim(every_key, first_row, window_rows, 0).astype(jnp.float32)
        key_block = key_block.reshape(window_rows, KV_HEADS, HEAD_DIM)
        value_block = lax.dynamic_slice_in_dim(every_value, first_row, window_rows, 0).astype(jnp.float32)
        value_block = value_block.reshape(window_rows, KV_HEADS, HEAD_DIM)
        scores = jnp.einsum("tkgd,skd->kgts", query_block, key_block) * score_scale
        query_pos = first_row + jnp.arange(block_rows, dtype=jnp.int32)
        key_pos = first_row - PAST + jnp.arange(window_rows, dtype=jnp.int32)
        distance_back = query_pos[:, None] - key_pos[None, :]
        visible = (distance_back >= 0) & (distance_back < WINDOW)
        scores = jnp.where(visible, scores, -jnp.inf)
        maxima = jnp.max(scores, axis=-1, keepdims=True)
        shifted = jnp.exp(scores - maxima)
        softmax_weights = (shifted / jnp.sum(shifted, axis=-1, keepdims=True)).astype(jnp.bfloat16)
        mixed_heads = jnp.einsum("kgts,skd->tkgd", softmax_weights.astype(jnp.float32), value_block)
        return mixed_heads.astype(jnp.bfloat16).reshape(block_rows, Q_HEADS * HEAD_DIM)

    block_ids = jnp.arange(TOKENS // TOK_DEV, dtype=jnp.int32)
    attended = lax.map(attend, block_ids).reshape(TOKENS, Q_HEADS * HEAD_DIM)
    share = Q_HEADS * HEAD_DIM // N_HEAD

    def add_group(group_index, total):
        rows_start = (group_index * share).astype(jnp.int32)
        attended_part = lax.dynamic_slice_in_dim(attended, rows_start, share, 1)
        weight_part = lax.dynamic_slice_in_dim(out_weight, rows_start, share, 0)
        return total + rounded(jnp.dot(attended_part, weight_part, preferred_element_type=jnp.float32))

    total = lax.fori_loop(0, N_HEAD, add_group, jnp.zeros((TOKENS, D), jnp.float32))
    return total.astype(jnp.bfloat16)
```

```python
import functools

import jax
import jax.numpy as jnp
from jax import lax
from jax.experimental import pallas as pl
from jax.experimental.pallas import tpu as pltpu
from jax.sharding import PartitionSpec as P

HEAD_DIM = 128
QUERY_SCALAR = 168
LOG2E = 1.4426950408889634
NZ = 8
NY = 8
BLK = 256
HALF = 128
KEYS = 5 * BLK
SPAN = 1024 + HALF
COLS = 336
PAD = 384
ROWS = 16
MESH = pl.DeviceIdType.MESH
DIST = (0, 1, -1, 2, -2, 3, -3, 4)
SLOT = {d: i for i, d in enumerate(DIST)}


def kernel(
    q_hbm, k_hbm, v_hbm, pk_hbm, pv_hbm, w_hbm, o_hbm,
    q, kv, wrow, wsrc, wfull, att, acc, xsend, xrecv, out,
    in_sem, past_sem, out_sem,
    kv_send, kv_recv, fwd_send,
    w1_send, w1_recv, wy_send, wy_recv, ws_send, ws_recv,
    z_send, z_recv, x_send, x_recv,
):
    c = lax.axis_index("ctx")
    h = lax.axis_index("head")
    n_ctx = lax.axis_size("ctx")
    core = lax.rem(c, 2)
    y = c // 4
    z = h // 2
    x_lo = lax.rem(h, 2)
    sibling = (c + 1 - 2 * core, h)
    partner = (c, h + 1 - 2 * x_lo)

    def at_z(d):
        return (c, lax.rem(z + d + NZ, NZ) * 2 + x_lo)

    def at_c(d):
        return (lax.rem(c + d + n_ctx, n_ctx), h)

    my_w = pl.ds(pl.multiple_of(y * 32 + core * ROWS, ROWS), ROWS)
    loads = [
        pltpu.make_async_copy(k_hbm, kv.at[0, pl.ds(4 * BLK, BLK)], in_sem.at[0]),
        pltpu.make_async_copy(v_hbm, kv.at[1, pl.ds(4 * BLK, BLK)], in_sem.at[1]),
        pltpu.make_async_copy(w_hbm.at[my_w], wrow, in_sem.at[2]),
        pltpu.make_async_copy(q_hbm, q, in_sem.at[3]),
    ]
    for copy in loads:
        copy.start()

    def past_copies(j):
        rows = pl.ds(pl.multiple_of(jnp.minimum(c + j, 3) * BLK, BLK), BLK)
        return (
            pltpu.make_async_copy(pk_hbm.at[rows], kv.at[0, pl.ds(j * BLK, BLK)], past_sem.at[2 * j]),
            pltpu.make_async_copy(pv_hbm.at[rows], kv.at[1, pl.ds(j * BLK, BLK)], past_sem.at[2 * j + 1]),
        )

    for j in range(4):
        @pl.when(c + j < 4)
        def _(j=j):
            for copy in past_copies(j):
                copy.start()

    barrier = pltpu.get_barrier_semaphore()
    partners = [at_z(d) for d in range(1, NZ)] + [at_c(d) for d in (-4, -2, 2, 4)] + [sibling, partner]
    for device in partners:
        pl.semaphore_signal(barrier, inc=1, device_id=device, device_id_type=MESH)

    loads[2].wait()
    fill = jnp.zeros((ROWS, PAD - COLS), jnp.bfloat16)
    for t in range(NZ):
        at = t * 2 * COLS
        wsrc[t] = jnp.concatenate(
            [wrow[:, at : at + COLS], fill, wrow[:, at + COLS : at + 2 * COLS], fill], axis=1
        )
    loads[0].wait()
    loads[1].wait()
    pl.semaphore_wait(barrier, len(partners))

    def remote(src, dst, send, recv, device):
        return pltpu.make_async_remote_copy(
            src_ref=src, dst_ref=dst, send_sem=send, recv_sem=recv, device_id=device, device_id_type=MESH
        )

    def kv_slot(j):
        return kv.at[:, pl.ds(pl.multiple_of(j * BLK, BLK), BLK)]

    def kv_copy(j, device, send):
        return remote(kv_slot(4), kv_slot(j), send, kv_recv.at[j], device)

    to_far = kv_copy(0, at_c(4), kv_send.at[0])
    to_near = kv_copy(2, at_c(2), kv_send.at[1])
    to_next = kv_copy(3, sibling, kv_send.at[2])

    @pl.when(c + 2 < n_ctx)
    def _():
        to_near.start()

    @pl.when(c + 4 < n_ctx)
    def _():
        to_far.start()

    @pl.when(core == 0)
    def _():
        to_next.start()

    def w1_copy(d):
        target = lax.rem(z - d + NZ, NZ)
        s = SLOT[d]
        return remote(wsrc.at[target], wfull.at[s, my_w], w1_send.at[s], w1_recv.at[s], at_z(-d))

    for d in DIST[1:]:
        w1_copy(d).start()
    wfull[0, my_w] = wsrc[z]

    near_slot = jnp.where(core == 0, 1, 3)
    fwd_near = remote(kv_slot(2), kv_slot(near_slot), fwd_send.at[0], kv_recv.at[near_slot], sibling)
    fwd_far = remote(kv_slot(0), kv_slot(1), fwd_send.at[1], kv_recv.at[1], sibling)

    def arrived(j):
        return remote(kv_slot(j), kv_slot(j), kv_send.at[0], kv_recv.at[j], sibling)

    @pl.when(c >= 4)
    def _():
        arrived(0).wait_recv()

    @pl.when((c >= 4) & (core == 1))
    def _():
        fwd_far.start()

    @pl.when(c >= 2)
    def _():
        arrived(2).wait_recv()
        fwd_near.start()

    def w_slab(part, dy, of_core):
        row = pl.multiple_of(lax.rem(y + dy + NY, NY) * 32 + of_core * ROWS, ROWS)
        return wfull.at[pl.ds(part * 4, 4), pl.ds(row, ROWS)]

    def wy_copy(part, way, step):
        slab = w_slab(part, -way * (step - 1), core)
        i = part * 8 + (way + 1) // 2 * 4 + step - 1
        return remote(slab, slab, wy_send.at[i], wy_recv.at[i], at_c(4 * way))

    def wy_arrived(part, way, step):
        slab = w_slab(part, -way * step, core)
        i = part * 8 + (way + 1) // 2 * 4 + step - 1
        return remote(slab, slab, wy_send.at[i], wy_recv.at[i], at_c(4 * way))

    def ws_copy(part, dy):
        slab = w_slab(part, dy, core)
        i = part * 8 + dy + 3
        return remote(slab, slab, ws_send.at[i], ws_recv.at[i], sibling)

    def ws_arrived(part, dy):
        slab = w_slab(part, dy, 1 - core)
        i = part * 8 + dy + 3
        return remote(slab, slab, ws_send.at[i], ws_recv.at[i], sibling)

    def last_way(part):
        return 1 if part == 0 else -1

    def w_start():
        for part in range(2):
            for s in range(max(1, part * 4), part * 4 + 4):
                w1_copy(DIST[s]).wait_recv()
            for way in (1, -1):
                wy_copy(part, way, 1).start()
            ws_copy(part, 0).start()

    def w_step(part, step):
        for way in (1, -1):
            if step == 4 and way != last_way(part):
                continue
            wy_arrived(part, way, step).wait_recv()
            if step < 3 or (step == 3 and way == last_way(part)):
                wy_copy(part, way, step + 1).start()
            ws_copy(part, 4 if step == 4 else -way * step).start()

    w_start()

    for j in range(4):
        @pl.when(c + j < 4)
        def _(j=j):
            for copy in past_copies(j):
                copy.wait()

    loads[3].wait()

    @pl.when((c >= 1) | (core == 1))
    def _():
        arrived(3).wait_recv()

    @pl.when(c >= 3)
    def _():
        arrived(1).wait_recv()

    factor = QUERY_SCALAR ** (-0.5) * LOG2E
    row = lax.broadcasted_iota(jnp.int32, (HALF, HALF), 0)
    col = lax.broadcasted_iota(jnp.int32, (HALF, HALF), 1)

    def attend(half):
        rows = pl.ds(half * HALF, HALF)
        keys = kv[0, half * HALF : half * HALF + SPAN]
        values = kv[1, half * HALF : half * HALF + SPAN]
        for g in range(2):
            head = pl.ds(g * HEAD_DIM, HEAD_DIM)
            s = lax.dot_general(
                q[rows, head], keys, (((1,), (1,)), ((), ())), preferred_element_type=jnp.float32
            )
            s = jnp.concatenate(
                [
                    jnp.where(col > row, s[:, :HALF], -jnp.inf),
                    s[:, HALF : SPAN - HALF],
                    jnp.where(col <= row, s[:, SPAN - HALF :], -jnp.inf),
                ],
                axis=1,
            )
            m = jnp.max(s, axis=1, keepdims=True)
            p = jnp.exp2((s - m) * factor)
            total = jnp.sum(p, axis=1, keepdims=True)
            mixed = jnp.dot(p.astype(jnp.bfloat16), values, preferred_element_type=jnp.float32)
            att[0, rows, head] = (mixed / total).astype(jnp.bfloat16)

    def z_copy(half, way, step):
        src, dst = SLOT[-way * (step - 1)], SLOT[4 if step == 4 else -way * step]
        rows = pl.ds(half * HALF, HALF)
        i = half * 8 + (way + 1) // 2 * 4 + step - 1
        return remote(att.at[src, rows], att.at[dst, rows], z_send.at[i], z_recv.at[i], at_z(way))

    def z_step(half, step):
        for way in (1, -1):
            if step == 4 and way != last_way(half):
                continue
            z_copy(half, way, step).wait_recv()
            if step < 3 or (step == 3 and way == last_way(half)):
                z_copy(half, way, step + 1).start()

    for half in range(2):
        attend(half)
        for way in (1, -1):
            z_copy(half, way, 1).start()

    w_step(0, 1)
    w_step(1, 1)
    z_step(0, 1)
    z_step(1, 1)
    z_step(0, 2)
    w_step(0, 2)
    z_step(1, 2)
    w_step(1, 2)
    z_step(0, 3)
    w_step(0, 3)
    z_step(1, 3)
    w_step(1, 3)

    def project(half, slots, first):
        rows = pl.ds(half * HALF, HALF)
        for s in slots:
            term = jnp.dot(att[s, rows, :], wfull[s], preferred_element_type=jnp.float32)
            if first and s == slots[0]:
                acc[rows, :] = term
            else:
                acc[rows, :] += term

    w_step(0, 4)
    w_step(1, 4)
    for part in range(2):
        for dy in range(-3, 5):
            ws_arrived(part, dy).wait_recv()

    def x_copy(half):
        rows = pl.ds(half * HALF, HALF)
        return remote(xsend.at[rows], xrecv.at[rows], x_send.at[half], x_recv.at[half], partner)

    mine = pl.ds(pl.multiple_of(x_lo * PAD, PAD), PAD)
    theirs = pl.ds(pl.multiple_of((1 - x_lo) * PAD, PAD), PAD)
    for half in range(2):
        rows = pl.ds(half * HALF, HALF)
        project(half, range(7), True)
        z_step(half, 4)
        project(half, range(7, 8), False)
        xsend[rows, :] = acc[rows, theirs].astype(jnp.bfloat16)
        x_copy(half).start()
    stores = []
    for half in range(2):
        rows = pl.ds(half * HALF, HALF)
        x_copy(half).wait_recv()
        both = acc[rows, mine] + xrecv[rows, :].astype(jnp.float32)
        out[rows, :] = both[:, :COLS].astype(jnp.bfloat16)
        store = pltpu.make_async_copy(out.at[rows], o_hbm.at[rows], out_sem.at[half])
        store.start()
        stores.append(store)

    @pl.when(c + 2 < n_ctx)
    def _():
        to_near.wait_send()

    @pl.when(c + 4 < n_ctx)
    def _():
        to_far.wait_send()

    @pl.when(core == 0)
    def _():
        to_next.wait_send()

    @pl.when(c >= 2)
    def _():
        fwd_near.wait_send()

    @pl.when((c >= 4) & (core == 1))
    def _():
        fwd_far.wait_send()

    for d in DIST[1:]:
        w1_copy(d).wait_send()
    for part in range(2):
        for way in (1, -1):
            for step in range(1, 5):
                if step < 4 or way == last_way(part):
                    wy_copy(part, way, step).wait_send()
                    z_copy(part, way, step).wait_send()
        for dy in range(-3, 5):
            ws_copy(part, dy).wait_send()
        x_copy(part).wait_send()
    for store in stores:
        store.wait()


def body(queries, key_states, value_states, past_keys, past_values, out_weight):
    bf16 = jnp.bfloat16
    dma = pltpu.SemaphoreType.DMA
    return pl.pallas_call(
        kernel,
        out_shape=jax.ShapeDtypeStruct((BLK, COLS), bf16),
        in_specs=[pl.BlockSpec(memory_space=pl.ANY)] * 6,
        out_specs=pl.BlockSpec(memory_space=pl.ANY),
        scratch_shapes=[
            pltpu.VMEM((BLK, 2 * HEAD_DIM), bf16),
            pltpu.VMEM((2, KEYS, HEAD_DIM), bf16),
            pltpu.VMEM((ROWS, out_weight.shape[1]), bf16),
            pltpu.VMEM((NZ, ROWS, 2 * PAD), bf16),
            pltpu.VMEM((NZ, BLK, 2 * PAD), bf16),
            pltpu.VMEM((NZ, BLK, 2 * HEAD_DIM), bf16),
            pltpu.VMEM((BLK, 2 * PAD), jnp.float32),
            pltpu.VMEM((BLK, PAD), bf16),
            pltpu.VMEM((BLK, PAD), bf16),
            pltpu.VMEM((BLK, COLS), bf16),
            dma((4,)), dma((8,)), dma((2,)),
            dma((3,)), dma((4,)), dma((2,)),
            dma((8,)), dma((8,)), dma((16,)), dma((16,)), dma((16,)), dma((16,)),
            dma((16,)), dma((16,)), dma((2,)), dma((2,)),
        ],
        compiler_params=pltpu.CompilerParams(
            collective_id=0, has_side_effects=True, vmem_limit_bytes=48 * 1024 * 1024
        ),
        cost_estimate=pl.CostEstimate(flops=10**9, bytes_accessed=4 * 10**6, transcendentals=700000),
    )(queries, key_states, value_states, past_keys, past_values, out_weight)


def solution(mesh):
    placed = (
        P("ctx", "head"),
        P("ctx", "head"),
        P("ctx", "head"),
        P(None, "head"),
        P(None, "head"),
        P("head", None),
    )
    return jax.shard_map(
        body, mesh=mesh, in_specs=placed, out_specs=P("ctx", "head"), check_vma=False
    )
```

```python
import jax
import jax.numpy as jnp
from jax import lax
from jax.experimental import pallas as pl
from jax.experimental.pallas import tpu as pltpu
from jax.sharding import PartitionSpec as P

HEAD_DIM = 128
QUERY_SCALAR = 168
LOG2E = 1.4426950408889634
NZ = 8
NY = 8
BLK = 256
HALF = 128
CHUNKS = 4
CHUNK = BLK // CHUNKS
KEYS = 5 * BLK
SPAN = 1024 + HALF
COLS = 336
TILES = 21
MAIN = 640
TAIL = 32
ROWS = 16
MESH = pl.DeviceIdType.MESH
DIST = (0, 1, -1, 2, -2, 3, -3, 4)
SLOT = {d: i for i, d in enumerate(DIST)}


def kernel(
    q_hbm, k_hbm, v_hbm, pk_hbm, pv_hbm, w_hbm, own_hbm, other_hbm,
    q, kv, wrow, wsrc, wstage, wfull, att, acc, acc_t, xsend,
    in_sem, past_sem, own_sem, kv_send, kv_recv, fwd_send,
    w1_send, w1_recv, wy_send, wy_recv, ws_send, ws_recv,
    z1_send, z1_recv, z_send, z_recv, z4_send, z4_recv, zs_send, zs_recv, x_send, x_recv,
):
    c = lax.axis_index("ctx")
    h = lax.axis_index("head")
    n_ctx = lax.axis_size("ctx")
    core = lax.rem(c, 2)
    c0 = c - core
    y = c // 4
    z = h // 2
    x_lo = lax.rem(h, 2)
    sibling = (c + 1 - 2 * core, h)
    partner = (c, h + 1 - 2 * x_lo)

    def at_z(d, of_core):
        return (c0 + of_core, lax.rem(z + d + NZ, NZ) * 2 + x_lo)

    def at_c(d):
        return (lax.rem(c + d + n_ctx, n_ctx), h)

    barrier = pltpu.get_barrier_semaphore()

    def greet(devices):
        for device in devices:
            pl.semaphore_signal(barrier, inc=1, device_id=device, device_id_type=MESH)

    def on_core(which):
        return pl.when(core == which)

    my_w = pl.ds(pl.multiple_of(y * 32 + core * ROWS, ROWS), ROWS)
    loads = [
        pltpu.make_async_copy(w_hbm.at[my_w], wrow, in_sem.at[0]),
        pltpu.make_async_copy(k_hbm, kv.at[0, pl.ds(4 * BLK, BLK)], in_sem.at[1]),
        pltpu.make_async_copy(v_hbm, kv.at[1, pl.ds(4 * BLK, BLK)], in_sem.at[2]),
        pltpu.make_async_copy(q_hbm, q, in_sem.at[3]),
    ]
    for copy in loads[:3]:
        copy.start()

    greet([sibling, partner, at_c(-2), at_c(-4)])
    greet([at_z(d, of_core) for d in (1, -1) for of_core in (0, 1)])

    @on_core(1)
    def _():
        greet([at_c(4)])
        greet([at_z(d, of_core) for d in range(2, NZ - 1) for of_core in (0, 1)])

    loads[3].start()

    def past_copies(j):
        rows = pl.ds(pl.multiple_of(jnp.minimum(c + j, 3) * BLK, BLK), BLK)
        return (
            pltpu.make_async_copy(pk_hbm.at[rows], kv.at[0, pl.ds(j * BLK, BLK)], past_sem.at[2 * j]),
            pltpu.make_async_copy(pv_hbm.at[rows], kv.at[1, pl.ds(j * BLK, BLK)], past_sem.at[2 * j + 1]),
        )

    def each_past(act):
        @pl.when(c < 4)
        def _():
            for j in range(4):
                @pl.when(c + j < 4)
                def _(j=j):
                    for copy in past_copies(j):
                        act(copy)

    each_past(lambda copy: copy.start())

    with jax.named_scope("weight_rows"):
        loads[0].wait()
    group = lax.broadcasted_iota(jnp.int32, (ROWS, 128), 1) // TAIL
    for t in range(NZ):
        d = lax.rem(z - t + NZ, NZ)
        s = jnp.where(d > 4, 2 * (NZ - d), jnp.maximum(2 * d - 1, 0))
        at = t * 2 * COLS
        for i in range(5):
            wsrc[s, i] = wrow[:, at + i * 128 : at + (i + 1) * 128]
        tail = jnp.concatenate([wrow[:, at + MAIN : at + 2 * COLS]] * 4, axis=1)
        wsrc[s, 5] = jnp.where(group == lax.rem(s, 4), tail, jnp.zeros_like(tail))
    loads[1].wait()
    loads[2].wait()
    with jax.named_scope("entry"):
        @on_core(0)
        def _():
            pl.semaphore_wait(barrier, 13)

        @on_core(1)
        def _():
            pl.semaphore_wait(barrier, 14)

    def remote(src, dst, send, recv, device):
        return pltpu.make_async_remote_copy(
            src_ref=src, dst_ref=dst, send_sem=send, recv_sem=recv, device_id=device, device_id_type=MESH
        )

    def kv_slot(j):
        return kv.at[:, pl.ds(pl.multiple_of(j * BLK, BLK), BLK)]

    def kv_copy(j, device, send):
        return remote(kv_slot(4), kv_slot(j), send, kv_recv.at[j], device)

    def kv_start(j, device, send):
        for i in range(2):
            remote(kv_slot(4).at[i], kv_slot(j).at[i], send, kv_recv.at[j], device).start()

    to_far = kv_copy(0, at_c(4), kv_send.at[0])
    to_near = kv_copy(2, at_c(2), kv_send.at[1])
    to_next = kv_copy(3, sibling, kv_send.at[2])

    @pl.when(c + 2 < n_ctx)
    def _():
        kv_start(2, at_c(2), kv_send.at[1])

    @pl.when(c + 4 < n_ctx)
    def _():
        kv_start(0, at_c(4), kv_send.at[0])

    @on_core(0)
    def _():
        to_next.start()

    def w1_copy(s, of_core):
        return remote(wsrc.at[s], wstage.at[of_core, s], w1_send.at[s], w1_recv.at[of_core * 8 + s], at_z(-DIST[s], 1))

    @on_core(0)
    def _():
        w1_copy(0, 0).start()

    for s in range(1, NZ):
        w1_copy(s, core).start()

    near_slot = jnp.where(core == 0, 1, 3)
    fwd_near = remote(kv_slot(2), kv_slot(near_slot), fwd_send.at[0], kv_recv.at[near_slot], sibling)
    fwd_far = remote(kv_slot(0), kv_slot(1), fwd_send.at[1], kv_recv.at[1], sibling)

    def arrived(j):
        return remote(kv_slot(j), kv_slot(j), kv_send.at[0], kv_recv.at[j], sibling)

    def w_slab(n, dy):
        row = pl.multiple_of(lax.rem(y + dy + NY, NY) * 32, 32)
        tiles = pl.ds(10, 11) if n % 2 else pl.ds(0, 10)
        return wfull.at[n // 2, tiles, pl.ds(row, 32)]

    def wy_sem(n, way, step):
        return n * 8 + (way + 1) // 2 * 4 + step - 1

    def wy_copy(n, way, step):
        slab = w_slab(n, -way * (step - 1))
        i = wy_sem(n, way, step)
        return remote(slab, slab, wy_send.at[i], wy_recv.at[i], at_c(4 * way))

    def wy_arrived(n, way, step):
        slab = w_slab(n, -way * step)
        i = wy_sem(n, way, step)
        return remote(slab, slab, wy_send.at[i], wy_recv.at[i], at_c(4 * way))

    def ws_copy(n, dy):
        slab = w_slab(n, dy)
        i = n * 8 + dy + 3
        return remote(slab, slab, ws_send.at[i], ws_recv.at[i], sibling)

    def last_way(part):
        return 1 if part == 0 else -1

    def w_start(n):
        part = n // 2
        for of_core in range(2):
            rows = pl.ds(pl.multiple_of(y * 32 + of_core * ROWS, ROWS), ROWS)

            def piece(j, i):
                own = part * 4 + j == 0 and of_core == 1
                return wsrc[0, i] if own else wstage[of_core, part * 4 + j, i]

            for j in (n % 2 * 2, n % 2 * 2 + 1):
                if part * 4 + j or of_core == 0:
                    w1_copy(part * 4 + j, of_core).wait_recv()
                for i in range(5):
                    wfull[part, j * 5 + i, rows] = piece(j, i)
            if n % 2:
                wfull[part, TILES - 1, rows] = piece(0, 5) + piece(1, 5) + piece(2, 5) + piece(3, 5)
        for way in (1, -1):
            wy_copy(n, way, 1).start()
        ws_copy(n, 0).start()

    def w_step(n, step):
        for way in (1, -1):
            if step == 4 and way != last_way(n % 2):
                continue
            wy_arrived(n, way, step).wait_recv()
            if step < 3 or (step == 3 and way == last_way(n % 2)):
                wy_copy(n, way, step + 1).start()
            ws_copy(n, 4 if step == 4 else -way * step).start()

    def weights(*todo):
        @on_core(1)
        def _():
            for n, step in todo:
                with jax.named_scope("weight_%d_hop_%d" % (n, step)):
                    w_step(n, step) if step else w_start(n)

    weights((0, 0))
    with jax.named_scope("far_block"):
        @pl.when(c >= 4)
        def _():
            arrived(0).wait_recv()

    @pl.when((c >= 4) & (core == 1))
    def _():
        fwd_far.start()

    weights((1, 0), (2, 0))
    with jax.named_scope("near_block"):
        @pl.when(c >= 2)
        def _():
            arrived(2).wait_recv()
            fwd_near.start()

    weights((3, 0), (0, 1))
    each_past(lambda copy: copy.wait())
    loads[3].wait()

    with jax.named_scope("passed_blocks"):
        @pl.when((c >= 1) | (core == 1))
        def _():
            arrived(3).wait_recv()

        @pl.when(c >= 3)
        def _():
            arrived(1).wait_recv()

    factor = QUERY_SCALAR ** (-0.5) * LOG2E
    row = lax.broadcasted_iota(jnp.int32, (HALF, HALF), 0)
    col = lax.broadcasted_iota(jnp.int32, (HALF, HALF), 1)

    def attend(half):
        rows = pl.ds(half * HALF, HALF)
        keys = kv[0, half * HALF : half * HALF + SPAN]
        values = kv[1, half * HALF : half * HALF + SPAN]
        for g in range(2):
            head = pl.ds(g * HEAD_DIM, HEAD_DIM)
            s = lax.dot_general(
                q[rows, head], keys, (((1,), (1,)), ((), ())), preferred_element_type=jnp.float32
            )
            s = jnp.concatenate(
                [
                    jnp.where(col > row, s[:, :HALF], -jnp.inf),
                    s[:, HALF : SPAN - HALF],
                    jnp.where(col <= row, s[:, SPAN - HALF :], -jnp.inf),
                ],
                axis=1,
            )
            m = jnp.max(s, axis=1, keepdims=True)
            p = jnp.exp2((s - m) * factor)
            total = jnp.sum(p, axis=1, keepdims=True)
            mixed = jnp.dot(p.astype(jnp.bfloat16), values, preferred_element_type=jnp.float32)
            att[core, 0, rows, head] = (mixed / total).astype(jnp.bfloat16)

    def rows_of(half):
        return pl.ds(half * HALF, HALF)

    def chunk_of(n):
        return pl.ds(n * CHUNK, CHUNK)

    def z1_copy(n, way, of_core):
        rows = chunk_of(n)
        k = n * 2 + (way + 1) // 2
        return remote(
            att.at[of_core, 0, rows], att.at[of_core, SLOT[-way], rows],
            z1_send.at[k], z1_recv.at[k * 2 + of_core], at_z(way, 0),
        )

    def z_copy(n, way, step, of_core):
        rows = chunk_of(n)
        i = ((n * 2 + (way + 1) // 2) * 2 + step - 2) * 2 + of_core
        return remote(
            att.at[of_core, SLOT[-way * (step - 1)], rows], att.at[of_core, SLOT[-way * step], rows],
            z_send.at[i], z_recv.at[i], at_z(way, 0),
        )

    def z4_copy(n, of_core):
        way = last_way(n % 2)
        rows = chunk_of(n)
        return remote(
            att.at[of_core, SLOT[-way * 3], rows], att.at[of_core, SLOT[4], rows],
            z4_send.at[n * 2 + of_core], z4_recv.at[n], at_z(way, of_core),
        )

    def zs_copy(n, slot):
        rows = chunk_of(n)
        i = n * 8 + slot
        return remote(att.at[1, slot, rows], att.at[1, slot, rows], zs_send.at[i], zs_recv.at[i], sibling)

    def z_step(n, step):
        for way in (-1, 1):
            for of_core in range(2):
                if step == 1:
                    z1_copy(n, way, of_core).wait_recv()
                else:
                    z_copy(n, way, step, of_core).wait_recv()
                if step < 3:
                    z_copy(n, way, step + 1, of_core).start()
                elif way == last_way(n % 2):
                    z4_copy(n, of_core).start()
            zs_copy(n, SLOT[-way * step]).start()

    for half in range(2):
        with jax.named_scope("attend_%d" % half):
            attend(half)
        for n in range(half * CHUNKS // 2, (half + 1) * CHUNKS // 2):
            for way in (1, -1):
                z1_copy(n, way, core).start()

    @on_core(0)
    def _():
        for step in range(1, 4):
            for n in range(CHUNKS):
                with jax.named_scope("attended_%d_hop_%d" % (n, step)):
                    z_step(n, step)
        with jax.named_scope("weights_from_core_1"):
            for n in range(4):
                for dy in range(-3, 5):
                    ws_copy(n, dy).wait_recv()

    weights(*[(n, step) for step in range(1, 5) for n in range(4) if (n, step) != (0, 1)])

    tail_of = lax.broadcasted_iota(jnp.int32, (HALF, 128), 1) // TAIL

    def project(half, slots):
        rows = rows_of(half)
        for s in slots:
            at = s % 4 * 5
            weight = jnp.concatenate(
                [wfull[s // 4, at + i] for i in range(5)] + [wfull[s // 4, TILES - 1]], axis=1
            )
            term = jnp.dot(att[core, s, rows, :], weight, preferred_element_type=jnp.float32)
            tail = jnp.where(tail_of == s % 4, term[:, MAIN:], 0.0)
            if s == 0:
                acc[rows, :MAIN] = term[:, :MAIN]
                acc[rows, MAIN:] = tail
            else:
                acc[rows, :MAIN] += term[:, :MAIN]
                acc[rows, MAIN:] += tail

    def x_copy(half):
        return remote(
            xsend.at[half], other_hbm.at[:, pl.ds(half * HALF, HALF)], x_send.at[half], x_recv.at[half], partner
        )

    def own_copy(half):
        mine = pl.ds(pl.multiple_of(x_lo * COLS, 16), COLS)
        return pltpu.make_async_copy(acc_t.at[half, mine], own_hbm.at[:, pl.ds(half * HALF, HALF)], own_sem.at[half])

    for half in range(2):
        rows = rows_of(half)
        with jax.named_scope("attended_from_core_0"):
            @on_core(1)
            def _(half=half):
                for n in range(half * CHUNKS // 2, (half + 1) * CHUNKS // 2):
                    for slot in range(1, 7):
                        zs_copy(n, slot).wait_recv()
        with jax.named_scope("project_%d" % half):
            project(half, range(7))
        with jax.named_scope("attended_%d_hop_4" % half):
            for n in range(half * CHUNKS // 2, (half + 1) * CHUNKS // 2):
                z4_copy(n, core).wait_recv()
        project(half, range(7, 8))
        tail = acc[rows, MAIN:].T
        acc_t[half, :MAIN] = acc[rows, :MAIN].T
        acc_t[half, MAIN:] = tail[:32] + tail[32:64] + tail[64:96] + tail[96:]
        theirs = pl.ds(pl.multiple_of((1 - x_lo) * COLS, 16), COLS)
        xsend[half] = acc_t[half, theirs].astype(jnp.bfloat16)
        x_copy(half).start()
        own_copy(half).start()

    with jax.named_scope("sent"):
        @pl.when(c + 2 < n_ctx)
        def _():
            to_near.wait_send()

        @pl.when(c + 4 < n_ctx)
        def _():
            to_far.wait_send()

        @pl.when(c >= 2)
        def _():
            fwd_near.wait_send()

        @pl.when((c >= 4) & (core == 1))
        def _():
            fwd_far.wait_send()

        for s in range(1, NZ):
            w1_copy(s, core).wait_send()
        for n in range(CHUNKS):
            for way in (1, -1):
                z1_copy(n, way, core).wait_send()

        @on_core(0)
        def _():
            to_next.wait_send()
            w1_copy(0, 0).wait_send()
            for n in range(CHUNKS):
                for of_core in range(2):
                    for way in (1, -1):
                        for step in (2, 3):
                            z_copy(n, way, step, of_core).wait_send()
                    z4_copy(n, of_core).wait_send()
                for slot in range(1, 7):
                    zs_copy(n, slot).wait_send()

        @on_core(1)
        def _():
            for n in range(4):
                for way in (1, -1):
                    for step in range(1, 5):
                        if step < 4 or way == last_way(n % 2):
                            wy_copy(n, way, step).wait_send()
                for dy in range(-3, 5):
                    ws_copy(n, dy).wait_send()

    with jax.named_scope("partner_sums"):
        for half in range(2):
            own_copy(half).wait()
            x_copy(half).wait()


def body(queries, key_states, value_states, past_keys, past_values, out_weight):
    bf16 = jnp.bfloat16
    dma = pltpu.SemaphoreType.DMA
    own, other = pl.pallas_call(
        kernel,
        out_shape=(jax.ShapeDtypeStruct((COLS, BLK), jnp.float32), jax.ShapeDtypeStruct((COLS, BLK), bf16)),
        in_specs=[pl.BlockSpec(memory_space=pl.ANY)] * 6,
        out_specs=(pl.BlockSpec(memory_space=pl.ANY),) * 2,
        scratch_shapes=[
            pltpu.VMEM((BLK, 2 * HEAD_DIM), bf16),
            pltpu.VMEM((2, KEYS, HEAD_DIM), bf16),
            pltpu.VMEM((ROWS, out_weight.shape[1]), bf16),
            pltpu.VMEM((NZ, 6, ROWS, 128), bf16),
            pltpu.VMEM((2, NZ, 6, ROWS, 128), bf16),
            pltpu.VMEM((2, TILES, BLK, 128), bf16),
            pltpu.VMEM((2, NZ, BLK, 2 * HEAD_DIM), bf16),
            pltpu.VMEM((BLK, MAIN + 128), jnp.float32),
            pltpu.VMEM((2, 2 * COLS, HALF), jnp.float32),
            pltpu.VMEM((2, COLS, HALF), bf16),
            dma((4,)), dma((8,)), dma((2,)), dma((3,)), dma((4,)), dma((2,)),
            dma((8,)), dma((16,)), dma((32,)), dma((32,)), dma((32,)), dma((32,)),
            dma((2 * CHUNKS,)), dma((4 * CHUNKS,)), dma((8 * CHUNKS,)), dma((8 * CHUNKS,)),
            dma((2 * CHUNKS,)), dma((CHUNKS,)), dma((8 * CHUNKS,)), dma((8 * CHUNKS,)), dma((2,)), dma((2,)),
        ],
        compiler_params=pltpu.CompilerParams(
            collective_id=0, has_side_effects=True, vmem_limit_bytes=63 * 1024 * 1024
        ),
        cost_estimate=pl.CostEstimate(flops=10**9, bytes_accessed=4 * 10**6, transcendentals=700000),
    )(queries, key_states, value_states, past_keys, past_values, out_weight)
    return (own + other.astype(jnp.float32)).astype(bf16).T


def solution(mesh):
    placed = (
        P("ctx", "head"),
        P("ctx", "head"),
        P("ctx", "head"),
        P(None, "head"),
        P(None, "head"),
        P("head", None),
    )
    return jax.shard_map(
        body, mesh=mesh, in_specs=placed, out_specs=P("ctx", "head"), check_vma=False
    )
```

```python
import jax
import jax.numpy as jnp
from jax import lax
from jax.experimental import pallas as pl
from jax.experimental.pallas import tpu as pltpu
from jax.sharding import PartitionSpec as P

HEAD_DIM = 128
QUERY_SCALAR = 168
LOG2E = 1.4426950408889634
NZ = 8
NY = 8
BLK = 256
HALF = 128
CHUNKS = 4
CHUNK = BLK // CHUNKS
KEYS = 5 * BLK
SPAN = 1024 + HALF
COLS = 336
TILES = 21
MAIN = 640
TAIL = 32
ROWS = 16
MESH = pl.DeviceIdType.MESH
DIST = (0, 1, -1, 2, -2, 3, -3, 4)
SLOT = {d: i for i, d in enumerate(DIST)}


def kernel(
    q_hbm, k_hbm, v_hbm, pk_hbm, pv_hbm, w_hbm, own_hbm, other_hbm,
    q, kv, wrow, wsrc, wstage, wfull, att, acc, acc_t, xsend,
    in_sem, past_sem, own_sem, kv_send, kv_recv, fwd_send,
    w1_send, w1_recv, wy_send, wy_recv, ws_send, ws_recv,
    z1_send, z_send, z_recv, z4_recv, zs_send, zs_recv, x_send, x_recv,
):
    c = lax.axis_index("ctx")
    h = lax.axis_index("head")
    n_ctx = lax.axis_size("ctx")
    core = lax.rem(c, 2)
    c0 = c - core
    y = c // 4
    z = h // 2
    x_lo = lax.rem(h, 2)
    sibling = (c + 1 - 2 * core, h)
    partner = (c, h + 1 - 2 * x_lo)

    def at_z(d, of_core):
        return (c0 + of_core, lax.rem(z + d + NZ, NZ) * 2 + x_lo)

    def at_c(d):
        return (lax.rem(c + d + n_ctx, n_ctx), h)

    barrier = pltpu.get_barrier_semaphore()

    def greet(devices):
        for device in devices:
            pl.semaphore_signal(barrier, inc=1, device_id=device, device_id_type=MESH)

    def on_core(which):
        return pl.when(core == which)

    my_w = pl.ds(pl.multiple_of(y * 32 + core * ROWS, ROWS), ROWS)
    loads = [
        pltpu.make_async_copy(w_hbm.at[my_w], wrow, in_sem.at[0]),
        pltpu.make_async_copy(k_hbm, kv.at[0, pl.ds(4 * BLK, BLK)], in_sem.at[1]),
        pltpu.make_async_copy(v_hbm, kv.at[1, pl.ds(4 * BLK, BLK)], in_sem.at[2]),
        pltpu.make_async_copy(q_hbm, q, in_sem.at[3]),
    ]
    for copy in loads[:3]:
        copy.start()

    greet([sibling, partner, at_c(-2), at_c(-4)])
    greet([at_z(d, of_core) for d in (1, -1) for of_core in (0, 1)])

    @on_core(1)
    def _():
        greet([at_c(4)])
        greet([at_z(d, of_core) for d in range(2, NZ - 1) for of_core in (0, 1)])

    loads[3].start()

    def each_past(act):
        for first in range(4):
            @pl.when(c == first)
            def _(first=first):
                there = pl.ds(first * BLK, (4 - first) * BLK)
                here = pl.ds(0, (4 - first) * BLK)
                act(pltpu.make_async_copy(pk_hbm.at[there], kv.at[0, here], past_sem.at[0]))
                act(pltpu.make_async_copy(pv_hbm.at[there], kv.at[1, here], past_sem.at[1]))

    each_past(lambda copy: copy.start())

    with jax.named_scope("weight_rows"):
        loads[0].wait()
    group = lax.broadcasted_iota(jnp.int32, (ROWS, 128), 1) // TAIL
    for t in range(NZ):
        d = lax.rem(z - t + NZ, NZ)
        s = jnp.where(d > 4, 2 * (NZ - d), jnp.maximum(2 * d - 1, 0))
        at = t * 2 * COLS
        for i in range(5):
            wsrc[s, i] = wrow[:, at + i * 128 : at + (i + 1) * 128]
        tail = jnp.concatenate([wrow[:, at + MAIN : at + 2 * COLS]] * 4, axis=1)
        wsrc[s, 5] = jnp.where(group == lax.rem(s, 4), tail, jnp.zeros_like(tail))
    loads[1].wait()
    loads[2].wait()
    with jax.named_scope("entry"):
        @on_core(0)
        def _():
            pl.semaphore_wait(barrier, 13)

        @on_core(1)
        def _():
            pl.semaphore_wait(barrier, 14)

    def remote(src, dst, send, recv, device):
        return pltpu.make_async_remote_copy(
            src_ref=src, dst_ref=dst, send_sem=send, recv_sem=recv, device_id=device, device_id_type=MESH
        )

    def all_of(ref, sem):
        return remote(ref, ref, sem, sem, sibling)

    def kv_slot(j):
        return kv.at[:, pl.ds(pl.multiple_of(j * BLK, BLK), BLK)]

    def kv_copy(j, device, send):
        return remote(kv_slot(4), kv_slot(j), send, kv_recv.at[j], device)

    def kv_start(j, device, send):
        for i in range(2):
            remote(kv_slot(4).at[i], kv_slot(j).at[i], send, kv_recv.at[j], device).start()

    to_far = kv_copy(0, at_c(4), kv_send.at[0])
    to_near = kv_copy(2, at_c(2), kv_send.at[1])
    to_next = kv_copy(3, sibling, kv_send.at[2])

    @pl.when(c + 2 < n_ctx)
    def _():
        kv_start(2, at_c(2), kv_send.at[1])

    @pl.when(c + 4 < n_ctx)
    def _():
        kv_start(0, at_c(4), kv_send.at[0])

    @on_core(0)
    def _():
        to_next.start()

    def w1_copy(s, of_core):
        return remote(wsrc.at[s], wstage.at[s, of_core], w1_send, w1_recv.at[s // 2], at_z(-DIST[s], 1))

    @on_core(0)
    def _():
        w1_copy(0, 0).start()

    for s in range(1, NZ):
        w1_copy(s, core).start()

    near_slot = jnp.where(core == 0, 1, 3)
    fwd_near = remote(kv_slot(2), kv_slot(near_slot), fwd_send.at[0], kv_recv.at[near_slot], sibling)
    fwd_far = remote(kv_slot(0), kv_slot(1), fwd_send.at[1], kv_recv.at[1], sibling)

    def arrived(j):
        return remote(kv_slot(j), kv_slot(j), kv_send.at[0], kv_recv.at[j], sibling)

    def w_slab(n, dy):
        row = pl.multiple_of(lax.rem(y + dy + NY, NY) * 32, 32)
        tiles = pl.ds(10, 11) if n % 2 else pl.ds(0, 10)
        return wfull.at[n // 2, tiles, pl.ds(row, 32)]

    def wy_sem(n, way, step):
        return n * 7 + (step - 1) * 2 + (way + 1) // 2 if step < 4 else n * 7 + 6

    def wy_copy(n, way, step):
        slab = w_slab(n, -way * (step - 1))
        i = wy_sem(n, way, step)
        return remote(slab, slab, wy_send, wy_recv.at[i], at_c(4 * way))

    def wy_arrived(n, way, step):
        slab = w_slab(n, -way * step)
        i = wy_sem(n, way, step)
        return remote(slab, slab, wy_send, wy_recv.at[i], at_c(4 * way))

    def ws_copy(n, dy):
        slab = w_slab(n, dy)
        return remote(slab, slab, ws_send, ws_recv, sibling)

    def last_way(part):
        return 1 if part == 0 else -1

    def w_start(n):
        part = n // 2
        if n == 0:
            all_of(wsrc.at[pl.ds(0, 3)], w1_recv.at[0]).wait_recv()
        else:
            all_of(wstage.at[pl.ds(n * 2, 2)], w1_recv.at[n]).wait_recv()
        for of_core in range(2):
            rows = pl.ds(pl.multiple_of(y * 32 + of_core * ROWS, ROWS), ROWS)

            def piece(j, i):
                own = part * 4 + j == 0 and of_core == 1
                return wsrc[0, i] if own else wstage[part * 4 + j, of_core, i]

            for j in (n % 2 * 2, n % 2 * 2 + 1):
                for i in range(5):
                    wfull[part, j * 5 + i, rows] = piece(j, i)
            if n % 2:
                wfull[part, TILES - 1, rows] = piece(0, 5) + piece(1, 5) + piece(2, 5) + piece(3, 5)
        for way in (1, -1):
            wy_copy(n, way, 1).start()
        ws_copy(n, 0).start()

    def w_step(n, step):
        for way in (1, -1):
            if step == 4 and way != last_way(n % 2):
                continue
            wy_arrived(n, way, step).wait_recv()
            if step < 3 or (step == 3 and way == last_way(n % 2)):
                wy_copy(n, way, step + 1).start()
            ws_copy(n, 4 if step == 4 else -way * step).start()

    def weights(*todo):
        @on_core(1)
        def _():
            for n, step in todo:
                with jax.named_scope("weight_%d_hop_%d" % (n, step)):
                    w_step(n, step) if step else w_start(n)

    def far_block():
        with jax.named_scope("far_block"):
            @pl.when(c >= 4)
            def _():
                arrived(0).wait_recv()

        @pl.when((c >= 4) & (core == 1))
        def _():
            fwd_far.start()

    def near_block():
        with jax.named_scope("near_block"):
            @pl.when(c >= 2)
            def _():
                arrived(2).wait_recv()
                fwd_near.start()

    near_first = (core == 0) | (lax.rem(c // 2, 2) == 1)
    weights((0, 0))
    pl.when(near_first)(near_block)
    pl.when(jnp.logical_not(near_first))(far_block)
    weights((1, 0), (2, 0))
    pl.when(near_first)(far_block)
    pl.when(jnp.logical_not(near_first))(near_block)
    weights((3, 0), (0, 1))
    each_past(lambda copy: copy.wait())
    loads[3].wait()

    with jax.named_scope("passed_blocks"):
        @pl.when((c >= 1) | (core == 1))
        def _():
            arrived(3).wait_recv()

        @pl.when(c >= 3)
        def _():
            arrived(1).wait_recv()

    factor = QUERY_SCALAR ** (-0.5) * LOG2E
    row = lax.broadcasted_iota(jnp.int32, (HALF, HALF), 0)
    col = lax.broadcasted_iota(jnp.int32, (HALF, HALF), 1)

    def attend(half):
        rows = pl.ds(half * HALF, HALF)
        keys = kv[0, half * HALF : half * HALF + SPAN]
        values = kv[1, half * HALF : half * HALF + SPAN]
        for g in range(2):
            head = pl.ds(g * HEAD_DIM, HEAD_DIM)
            s = lax.dot_general(
                q[rows, head], keys, (((1,), (1,)), ((), ())), preferred_element_type=jnp.float32
            )
            s = jnp.concatenate(
                [
                    jnp.where(col > row, s[:, :HALF], -jnp.inf),
                    s[:, HALF : SPAN - HALF],
                    jnp.where(col <= row, s[:, SPAN - HALF :], -jnp.inf),
                ],
                axis=1,
            )
            m = jnp.max(s, axis=1, keepdims=True)
            p = jnp.exp2((s - m) * factor)
            total = jnp.sum(p, axis=1, keepdims=True)
            mixed = jnp.dot(p.astype(jnp.bfloat16), values, preferred_element_type=jnp.float32)
            att[core, 0, rows, head] = (mixed / total).astype(jnp.bfloat16)

    def rows_of(half):
        return pl.ds(half * HALF, HALF)

    def chunk_of(n):
        return pl.ds(n * CHUNK, CHUNK)

    def z_sem(n, way, step):
        return (n * 3 + step - 1) * 2 + (way + 1) // 2

    def z1_copy(n, way, of_core):
        rows = chunk_of(n)
        return remote(
            att.at[of_core, 0, rows], att.at[of_core, SLOT[-way], rows],
            z1_send, z_recv.at[z_sem(n, way, 1)], at_z(way, 0),
        )

    def z_copy(n, way, step):
        rows = chunk_of(n)
        return remote(
            att.at[:, SLOT[-way * (step - 1)], rows], att.at[:, SLOT[-way * step], rows],
            z_send, z_recv.at[z_sem(n, way, step)], at_z(way, 0),
        )

    def z4_copy(n, of_core):
        way = last_way(n % 2)
        rows = chunk_of(n)
        return remote(
            att.at[of_core, SLOT[-way * 3], rows], att.at[of_core, SLOT[4], rows],
            z_send, z4_recv.at[n], at_z(way, of_core),
        )

    def zs_copy(n, slot):
        rows = chunk_of(n)
        return remote(att.at[1, slot, rows], att.at[1, slot, rows], zs_send, zs_recv.at[n * 2 // CHUNKS], sibling)

    def z_step(n, step):
        for way in (-1, 1):
            here = att.at[:, SLOT[-way * step], chunk_of(n)]
            all_of(here, z_recv.at[z_sem(n, way, step)]).wait_recv()
            if step < 3:
                z_copy(n, way, step + 1).start()
            elif way == last_way(n % 2):
                for of_core in range(2):
                    z4_copy(n, of_core).start()
            zs_copy(n, SLOT[-way * step]).start()

    for half in range(2):
        with jax.named_scope("attend_%d" % half):
            attend(half)
        for n in range(half * CHUNKS // 2, (half + 1) * CHUNKS // 2):
            for way in (1, -1):
                z1_copy(n, way, core).start()

    @on_core(0)
    def _():
        for step in range(1, 4):
            for n in range(CHUNKS):
                with jax.named_scope("attended_%d_hop_%d" % (n, step)):
                    z_step(n, step)
        with jax.named_scope("weights_from_core_1"):
            all_of(wfull, ws_recv).wait_recv()

    weights(*[(n, step) for step in range(1, 5) for n in range(4) if (n, step) != (0, 1)])

    tail_of = lax.broadcasted_iota(jnp.int32, (HALF, 128), 1) // TAIL

    def project(half, slots):
        rows = rows_of(half)
        for s in slots:
            at = s % 4 * 5
            weight = jnp.concatenate(
                [wfull[s // 4, at + i] for i in range(5)] + [wfull[s // 4, TILES - 1]], axis=1
            )
            term = jnp.dot(att[core, s, rows, :], weight, preferred_element_type=jnp.float32)
            tail = jnp.where(tail_of == s % 4, term[:, MAIN:], 0.0)
            if s == 0:
                acc[rows, :MAIN] = term[:, :MAIN]
                acc[rows, MAIN:] = tail
            else:
                acc[rows, :MAIN] += term[:, :MAIN]
                acc[rows, MAIN:] += tail

    def x_copy(half):
        return remote(
            xsend.at[half], other_hbm.at[:, pl.ds(half * HALF, HALF)], x_send.at[half], x_recv.at[half], partner
        )

    def own_copy(half):
        mine = pl.ds(pl.multiple_of(x_lo * COLS, 16), COLS)
        return pltpu.make_async_copy(acc_t.at[half, mine], own_hbm.at[:, pl.ds(half * HALF, HALF)], own_sem.at[half])

    for half in range(2):
        rows = rows_of(half)
        with jax.named_scope("attended_from_core_0"):
            @on_core(1)
            def _(half=half):
                all_of(att.at[1, pl.ds(1, 6), rows_of(half)], zs_recv.at[half]).wait_recv()
        with jax.named_scope("project_%d" % half):
            project(half, range(7))
        with jax.named_scope("attended_%d_hop_4" % half):
            for n in range(half * CHUNKS // 2, (half + 1) * CHUNKS // 2):
                z4_copy(n, core).wait_recv()
        project(half, range(7, 8))
        tail = acc[rows, MAIN:].T
        acc_t[half, :MAIN] = acc[rows, :MAIN].T
        acc_t[half, MAIN:] = tail[:32] + tail[32:64] + tail[64:96] + tail[96:]
        theirs = pl.ds(pl.multiple_of((1 - x_lo) * COLS, 16), COLS)
        xsend[half] = acc_t[half, theirs].astype(jnp.bfloat16)
        x_copy(half).start()
        own_copy(half).start()

    with jax.named_scope("sent"):
        @pl.when(c + 2 < n_ctx)
        def _():
            to_near.wait_send()

        @pl.when(c + 4 < n_ctx)
        def _():
            to_far.wait_send()

        @pl.when(c >= 2)
        def _():
            fwd_near.wait_send()

        @pl.when((c >= 4) & (core == 1))
        def _():
            fwd_far.wait_send()

        all_of(att.at[0, pl.ds(0, 2)], z1_send).wait_send()

        @on_core(0)
        def _():
            to_next.wait_send()
            all_of(wsrc, w1_send).wait_send()
            all_of(att.at[:, pl.ds(0, 5)], z_send).wait_send()
            all_of(att.at[1, pl.ds(0, 6)], zs_send).wait_send()

        @on_core(1)
        def _():
            all_of(wsrc.at[pl.ds(0, 7)], w1_send).wait_send()
            all_of(wfull.at[:, :, pl.ds(0, 7 * 32)], wy_send).wait_send()
            all_of(wfull, ws_send).wait_send()

    with jax.named_scope("partner_sums"):
        for half in range(2):
            own_copy(half).wait()
            x_copy(half).wait()


def body(queries, key_states, value_states, past_keys, past_values, out_weight):
    bf16 = jnp.bfloat16
    dma = pltpu.SemaphoreType.DMA
    own, other = pl.pallas_call(
        kernel,
        out_shape=(jax.ShapeDtypeStruct((COLS, BLK), jnp.float32), jax.ShapeDtypeStruct((COLS, BLK), bf16)),
        in_specs=[pl.BlockSpec(memory_space=pl.ANY)] * 6,
        out_specs=(pl.BlockSpec(memory_space=pl.ANY),) * 2,
        scratch_shapes=[
            pltpu.VMEM((BLK, 2 * HEAD_DIM), bf16),
            pltpu.VMEM((2, KEYS, HEAD_DIM), bf16),
            pltpu.VMEM((ROWS, out_weight.shape[1]), bf16),
            pltpu.VMEM((NZ, 6, ROWS, 128), bf16),
            pltpu.VMEM((NZ, 2, 6, ROWS, 128), bf16),
            pltpu.VMEM((2, TILES, BLK, 128), bf16),
            pltpu.VMEM((2, NZ, BLK, 2 * HEAD_DIM), bf16),
            pltpu.VMEM((BLK, MAIN + 128), jnp.float32),
            pltpu.VMEM((2, 2 * COLS, HALF), jnp.float32),
            pltpu.VMEM((2, COLS, HALF), bf16),
            dma((4,)), dma((2,)), dma((2,)), dma((3,)), dma((4,)), dma((2,)),
            dma(()), dma((4,)), dma(()), dma((28,)), dma(()), dma(()),
            dma(()), dma(()), dma((6 * CHUNKS,)), dma((CHUNKS,)), dma(()), dma((2,)), dma((2,)), dma((2,)),
        ],
        compiler_params=pltpu.CompilerParams(
            collective_id=0, has_side_effects=True, vmem_limit_bytes=63 * 1024 * 1024
        ),
        cost_estimate=pl.CostEstimate(flops=10**9, bytes_accessed=4 * 10**6, transcendentals=700000),
    )(queries, key_states, value_states, past_keys, past_values, out_weight)
    return (own + other.astype(jnp.float32)).astype(bf16).T


def solution(mesh):
    placed = (
        P("ctx", "head"),
        P("ctx", "head"),
        P("ctx", "head"),
        P(None, "head"),
        P(None, "head"),
        P("head", None),
    )
    return jax.shard_map(
        body, mesh=mesh, in_specs=placed, out_specs=P("ctx", "head"), check_vma=False
    )
```

```python
import jax
import jax.numpy as jnp
from jax import lax
from jax.experimental import pallas as pl
from jax.experimental.pallas import tpu as pltpu
from jax.sharding import PartitionSpec as P

HEAD_DIM = 128
QUERY_SCALAR = 168
LOG2E = 1.4426950408889634
NZ = 8
NY = 8
BLK = 256
HALF = 128
CHUNKS = 4
CHUNK = BLK // CHUNKS
KEYS = 5 * BLK
SPAN = 1024 + HALF
COLS = 336
TILES = 21
MAIN = 640
TAIL = 32
ROWS = 16
MESH = pl.DeviceIdType.MESH
DIST = (0, 1, -1, 2, -2, 3, -3, 4)
SLOT = {d: i for i, d in enumerate(DIST)}


def kernel(
    q_hbm, k_hbm, v_hbm, pk_hbm, pv_hbm, w_hbm, own_hbm, other_hbm,
    q, kv, wrow, wsrc, wstage, wfull, att, acc, acc_t, xsend,
    in_sem, past_sem, own_sem, kv_send, kv_recv, fwd_send,
    w1_send, w1_recv, wy_send, wy_recv, ws_send, ws_recv,
    z1_send, z_send, z_recv, z4_recv, zs_send, zs_recv, x_send, x_recv,
):
    c = lax.axis_index("ctx")
    h = lax.axis_index("head")
    n_ctx = lax.axis_size("ctx")
    core = lax.rem(c, 2)
    c0 = c - core
    y = c // 4
    z = h // 2
    x_lo = lax.rem(h, 2)
    sibling = (c + 1 - 2 * core, h)
    partner = (c, h + 1 - 2 * x_lo)

    def at_z(d, of_core):
        return (c0 + of_core, lax.rem(z + d + NZ, NZ) * 2 + x_lo)

    def at_c(d):
        return (lax.rem(c + d + n_ctx, n_ctx), h)

    barrier = pltpu.get_barrier_semaphore()

    def greet(devices):
        for device in devices:
            pl.semaphore_signal(barrier, inc=1, device_id=device, device_id_type=MESH)

    def on_core(which):
        return pl.when(core == which)

    my_w = pl.ds(pl.multiple_of(y * 32 + core * ROWS, ROWS), ROWS)
    loads = [
        pltpu.make_async_copy(w_hbm.at[my_w], wrow, in_sem.at[0]),
        pltpu.make_async_copy(k_hbm, kv.at[0, pl.ds(4 * BLK, BLK)], in_sem.at[1]),
        pltpu.make_async_copy(v_hbm, kv.at[1, pl.ds(4 * BLK, BLK)], in_sem.at[2]),
        pltpu.make_async_copy(q_hbm, q, in_sem.at[3]),
    ]
    greet([sibling, partner, at_c(-2), at_c(-4)])
    greet([at_z(d, of_core) for d in (1, -1) for of_core in (0, 1)])

    @on_core(1)
    def _():
        greet([at_c(4)])
        greet([at_z(d, of_core) for d in range(2, NZ - 1) for of_core in (0, 1)])

    for copy in loads:
        copy.start()

    def each_past(act):
        for first in range(4):
            @pl.when(c == first)
            def _(first=first):
                there = pl.ds(first * BLK, (4 - first) * BLK)
                here = pl.ds(0, (4 - first) * BLK)
                act(pltpu.make_async_copy(pk_hbm.at[there], kv.at[0, here], past_sem.at[0]))
                act(pltpu.make_async_copy(pv_hbm.at[there], kv.at[1, here], past_sem.at[1]))

    each_past(lambda copy: copy.start())

    with jax.named_scope("weight_rows"):
        loads[0].wait()
    group = lax.broadcasted_iota(jnp.int32, (ROWS, 128), 1) // TAIL
    for t in range(NZ):
        d = lax.rem(z - t + NZ, NZ)
        s = jnp.where(d > 4, 2 * (NZ - d), jnp.maximum(2 * d - 1, 0))
        at = t * 2 * COLS
        for i in range(5):
            wsrc[s, i] = wrow[:, at + i * 128 : at + (i + 1) * 128]
        tail = jnp.concatenate([wrow[:, at + MAIN : at + 2 * COLS]] * 4, axis=1)
        wsrc[s, 5] = jnp.where(group == lax.rem(s, 4), tail, jnp.zeros_like(tail))
    loads[1].wait()
    loads[2].wait()
    with jax.named_scope("entry"):
        @on_core(0)
        def _():
            pl.semaphore_wait(barrier, 13)

        @on_core(1)
        def _():
            pl.semaphore_wait(barrier, 14)

    def remote(src, dst, send, recv, device):
        return pltpu.make_async_remote_copy(
            src_ref=src, dst_ref=dst, send_sem=send, recv_sem=recv, device_id=device, device_id_type=MESH
        )

    def all_of(ref, sem):
        return remote(ref, ref, sem, sem, sibling)

    def kv_slot(j):
        return kv.at[:, pl.ds(pl.multiple_of(j * BLK, BLK), BLK)]

    def kv_copy(j, device, send):
        return remote(kv_slot(4), kv_slot(j), send, kv_recv.at[j], device)

    def kv_start(j, device, send):
        for i in range(2):
            remote(kv_slot(4).at[i], kv_slot(j).at[i], send, kv_recv.at[j], device).start()

    to_far = kv_copy(0, at_c(4), kv_send.at[0])
    to_near = kv_copy(2, at_c(2), kv_send.at[1])
    to_next = kv_copy(3, sibling, kv_send.at[2])

    @pl.when(c + 2 < n_ctx)
    def _():
        kv_start(2, at_c(2), kv_send.at[1])

    @pl.when(c + 4 < n_ctx)
    def _():
        kv_start(0, at_c(4), kv_send.at[0])

    @on_core(0)
    def _():
        to_next.start()

    def w1_copy(s, of_core):
        return remote(wsrc.at[s], wstage.at[s, of_core], w1_send, w1_recv.at[s // 2], at_z(-DIST[s], 1))

    @on_core(0)
    def _():
        w1_copy(0, 0).start()

    for s in range(1, NZ):
        w1_copy(s, core).start()

    near_slot = jnp.where(core == 0, 1, 3)
    fwd_near = remote(kv_slot(2), kv_slot(near_slot), fwd_send.at[0], kv_recv.at[near_slot], sibling)
    fwd_far = remote(kv_slot(0), kv_slot(1), fwd_send.at[1], kv_recv.at[1], sibling)

    def arrived(j):
        return remote(kv_slot(j), kv_slot(j), kv_send.at[0], kv_recv.at[j], sibling)

    def w_slab(n, dy):
        row = pl.multiple_of(lax.rem(y + dy + NY, NY) * 32, 32)
        tiles = pl.ds(10, 11) if n % 2 else pl.ds(0, 10)
        return wfull.at[n // 2, tiles, pl.ds(row, 32)]

    def wy_sem(n, way, step):
        return n * 7 + (step - 1) * 2 + (way + 1) // 2 if step < 4 else n * 7 + 6

    def wy_copy(n, way, step):
        slab = w_slab(n, -way * (step - 1))
        i = wy_sem(n, way, step)
        return remote(slab, slab, wy_send, wy_recv.at[i], at_c(4 * way))

    def wy_arrived(n, way, step):
        slab = w_slab(n, -way * step)
        i = wy_sem(n, way, step)
        return remote(slab, slab, wy_send, wy_recv.at[i], at_c(4 * way))

    def ws_copy(n, dy):
        slab = w_slab(n, dy)
        return remote(slab, slab, ws_send, ws_recv, sibling)

    def last_way(part):
        return 1 if part == 0 else -1

    def w_start(n):
        part = n // 2
        if n == 0:
            all_of(wsrc.at[pl.ds(0, 3)], w1_recv.at[0]).wait_recv()
        else:
            all_of(wstage.at[pl.ds(n * 2, 2)], w1_recv.at[n]).wait_recv()
        for of_core in range(2):
            rows = pl.ds(pl.multiple_of(y * 32 + of_core * ROWS, ROWS), ROWS)

            def piece(j, i):
                own = part * 4 + j == 0 and of_core == 1
                return wsrc[0, i] if own else wstage[part * 4 + j, of_core, i]

            for j in (n % 2 * 2, n % 2 * 2 + 1):
                for i in range(5):
                    wfull[part, j * 5 + i, rows] = piece(j, i)
            if n % 2:
                wfull[part, TILES - 1, rows] = piece(0, 5) + piece(1, 5) + piece(2, 5) + piece(3, 5)
        for way in (1, -1):
            wy_copy(n, way, 1).start()
        ws_copy(n, 0).start()

    def w_step(n, step):
        for way in (1, -1):
            if step == 4 and way != last_way(n % 2):
                continue
            wy_arrived(n, way, step).wait_recv()
            if step < 3 or (step == 3 and way == last_way(n % 2)):
                wy_copy(n, way, step + 1).start()
            ws_copy(n, 4 if step == 4 else -way * step).start()

    def weights(*todo):
        @on_core(1)
        def _():
            for n, step in todo:
                with jax.named_scope("weight_%d_hop_%d" % (n, step)):
                    w_step(n, step) if step else w_start(n)

    def far_block():
        with jax.named_scope("far_block"):
            @pl.when(c >= 4)
            def _():
                arrived(0).wait_recv()

        @pl.when((c >= 4) & (core == 1))
        def _():
            fwd_far.start()

    def near_block():
        with jax.named_scope("near_block"):
            @pl.when(c >= 2)
            def _():
                arrived(2).wait_recv()
                fwd_near.start()

    near_first = (core == 0) | (lax.rem(c // 2, 2) == 1)
    weights((0, 0))
    pl.when(near_first)(near_block)
    pl.when(jnp.logical_not(near_first))(far_block)
    weights((1, 0), (2, 0))
    pl.when(near_first)(far_block)
    pl.when(jnp.logical_not(near_first))(near_block)
    weights((3, 0), (0, 1))
    each_past(lambda copy: copy.wait())
    loads[3].wait()

    with jax.named_scope("passed_blocks"):
        @pl.when((c >= 1) | (core == 1))
        def _():
            arrived(3).wait_recv()

        @pl.when(c >= 3)
        def _():
            arrived(1).wait_recv()

    factor = QUERY_SCALAR ** (-0.5) * LOG2E
    row = lax.rem(lax.broadcasted_iota(jnp.int32, (2 * HALF, HALF), 0), HALF)
    col = lax.broadcasted_iota(jnp.int32, (2 * HALF, HALF), 1)

    def attend(half):
        rows = pl.ds(half * HALF, HALF)
        keys = kv[0, half * HALF : half * HALF + SPAN]
        values = kv[1, half * HALF : half * HALF + SPAN]
        both = jnp.concatenate([q[rows, :HEAD_DIM], q[rows, HEAD_DIM:]], axis=0)
        s = lax.dot_general(both, keys, (((1,), (1,)), ((), ())), preferred_element_type=jnp.float32)
        s = jnp.concatenate(
            [
                jnp.where(col > row, s[:, :HALF], -jnp.inf),
                s[:, HALF : SPAN - HALF],
                jnp.where(col <= row, s[:, SPAN - HALF :], -jnp.inf),
            ],
            axis=1,
        )
        m = jnp.max(s, axis=1, keepdims=True)
        p = jnp.exp2((s - m) * factor)
        total = jnp.sum(p, axis=1, keepdims=True)
        mixed = jnp.dot(p.astype(jnp.bfloat16), values, preferred_element_type=jnp.float32)
        mixed = (mixed * (1.0 / total)).astype(jnp.bfloat16)
        att[core, 0, rows, :HEAD_DIM] = mixed[:HALF]
        att[core, 0, rows, HEAD_DIM:] = mixed[HALF:]

    def rows_of(half):
        return pl.ds(half * HALF, HALF)

    def chunk_of(n):
        return pl.ds(n * CHUNK, CHUNK)

    def z_sem(n, way, step):
        return (n * 3 + step - 1) * 2 + (way + 1) // 2

    def z1_copy(n, way, of_core):
        rows = chunk_of(n)
        return remote(
            att.at[of_core, 0, rows], att.at[of_core, SLOT[-way], rows],
            z1_send, z_recv.at[z_sem(n, way, 1)], at_z(way, 0),
        )

    def z_copy(n, way, step):
        rows = chunk_of(n)
        return remote(
            att.at[:, SLOT[-way * (step - 1)], rows], att.at[:, SLOT[-way * step], rows],
            z_send, z_recv.at[z_sem(n, way, step)], at_z(way, 0),
        )

    def z4_copy(n, of_core):
        way = last_way(n % 2)
        rows = chunk_of(n)
        return remote(
            att.at[of_core, SLOT[-way * 3], rows], att.at[of_core, SLOT[4], rows],
            z_send, z4_recv.at[n], at_z(way, of_core),
        )

    def zs_copy(n, slot):
        rows = chunk_of(n)
        return remote(att.at[1, slot, rows], att.at[1, slot, rows], zs_send, zs_recv.at[n * 2 // CHUNKS], sibling)

    def z_step(n, step):
        for way in (-1, 1):
            here = att.at[:, SLOT[-way * step], chunk_of(n)]
            all_of(here, z_recv.at[z_sem(n, way, step)]).wait_recv()
            if step < 3:
                z_copy(n, way, step + 1).start()
            elif way == last_way(n % 2):
                for of_core in range(2):
                    z4_copy(n, of_core).start()
            zs_copy(n, SLOT[-way * step]).start()

    for half in range(2):
        with jax.named_scope("attend_%d" % half):
            attend(half)
        for n in range(half * CHUNKS // 2, (half + 1) * CHUNKS // 2):
            for way in (1, -1):
                z1_copy(n, way, core).start()

    @on_core(0)
    def _():
        for step in range(1, 4):
            for n in range(CHUNKS):
                with jax.named_scope("attended_%d_hop_%d" % (n, step)):
                    z_step(n, step)
        with jax.named_scope("weights_from_core_1"):
            all_of(wfull, ws_recv).wait_recv()

    weights(*[(n, step) for step in range(1, 5) for n in range(4) if (n, step) != (0, 1)])

    tail_of = lax.broadcasted_iota(jnp.int32, (HALF, 128), 1) // TAIL

    def project(half, slots):
        rows = rows_of(half)
        for s in slots:
            at = s % 4 * 5
            weight = jnp.concatenate(
                [wfull[s // 4, at + i] for i in range(5)] + [wfull[s // 4, TILES - 1]], axis=1
            )
            term = jnp.dot(att[core, s, rows, :], weight, preferred_element_type=jnp.float32)
            tail = jnp.where(tail_of == s % 4, term[:, MAIN:], 0.0)
            if s == 0:
                acc[rows, :MAIN] = term[:, :MAIN]
                acc[rows, MAIN:] = tail
            else:
                acc[rows, :MAIN] += term[:, :MAIN]
                acc[rows, MAIN:] += tail

    def x_copy(half):
        return remote(
            xsend.at[half], other_hbm.at[:, pl.ds(half * HALF, HALF)], x_send.at[half], x_recv.at[half], partner
        )

    def own_copy(half):
        mine = pl.ds(pl.multiple_of(x_lo * COLS, 16), COLS)
        return pltpu.make_async_copy(acc_t.at[half, mine], own_hbm.at[:, pl.ds(half * HALF, HALF)], own_sem.at[half])

    for half in range(2):
        rows = rows_of(half)
        with jax.named_scope("attended_from_core_0"):
            @on_core(1)
            def _(half=half):
                all_of(att.at[1, pl.ds(1, 6), rows_of(half)], zs_recv.at[half]).wait_recv()
        with jax.named_scope("project_%d" % half):
            project(half, range(7))
        with jax.named_scope("attended_%d_hop_4" % half):
            for n in range(half * CHUNKS // 2, (half + 1) * CHUNKS // 2):
                z4_copy(n, core).wait_recv()
        project(half, range(7, 8))
        tail = acc[rows, MAIN:].T
        acc_t[half, :MAIN] = acc[rows, :MAIN].T
        acc_t[half, MAIN:] = tail[:32] + tail[32:64] + tail[64:96] + tail[96:]
        theirs = pl.ds(pl.multiple_of((1 - x_lo) * COLS, 16), COLS)
        xsend[half] = acc_t[half, theirs].astype(jnp.bfloat16)
        x_copy(half).start()
        own_copy(half).start()

    with jax.named_scope("sent"):
        @pl.when(c + 2 < n_ctx)
        def _():
            to_near.wait_send()

        @pl.when(c + 4 < n_ctx)
        def _():
            to_far.wait_send()

        @pl.when(c >= 2)
        def _():
            fwd_near.wait_send()

        @pl.when((c >= 4) & (core == 1))
        def _():
            fwd_far.wait_send()

        all_of(att.at[0, pl.ds(0, 2)], z1_send).wait_send()

        @on_core(0)
        def _():
            to_next.wait_send()
            all_of(wsrc, w1_send).wait_send()
            all_of(att.at[:, pl.ds(0, 5)], z_send).wait_send()
            all_of(att.at[1, pl.ds(0, 6)], zs_send).wait_send()

        @on_core(1)
        def _():
            all_of(wsrc.at[pl.ds(0, 7)], w1_send).wait_send()
            all_of(wfull.at[:, :, pl.ds(0, 7 * 32)], wy_send).wait_send()
            all_of(wfull, ws_send).wait_send()

    with jax.named_scope("partner_sums"):
        for half in range(2):
            own_copy(half).wait()
            x_copy(half).wait()


def body(queries, key_states, value_states, past_keys, past_values, out_weight):
    bf16 = jnp.bfloat16
    dma = pltpu.SemaphoreType.DMA
    own, other = pl.pallas_call(
        kernel,
        out_shape=(jax.ShapeDtypeStruct((COLS, BLK), jnp.float32), jax.ShapeDtypeStruct((COLS, BLK), bf16)),
        in_specs=[pl.BlockSpec(memory_space=pl.ANY)] * 6,
        out_specs=(pl.BlockSpec(memory_space=pl.ANY),) * 2,
        scratch_shapes=[
            pltpu.VMEM((BLK, 2 * HEAD_DIM), bf16),
            pltpu.VMEM((2, KEYS, HEAD_DIM), bf16),
            pltpu.VMEM((ROWS, out_weight.shape[1]), bf16),
            pltpu.VMEM((NZ, 6, ROWS, 128), bf16),
            pltpu.VMEM((NZ, 2, 6, ROWS, 128), bf16),
            pltpu.VMEM((2, TILES, BLK, 128), bf16),
            pltpu.VMEM((2, NZ, BLK, 2 * HEAD_DIM), bf16),
            pltpu.VMEM((BLK, MAIN + 128), jnp.float32),
            pltpu.VMEM((2, 2 * COLS, HALF), jnp.float32),
            pltpu.VMEM((2, COLS, HALF), bf16),
            dma((4,)), dma((2,)), dma((2,)), dma((3,)), dma((4,)), dma((2,)),
            dma(()), dma((4,)), dma(()), dma((28,)), dma(()), dma(()),
            dma(()), dma(()), dma((6 * CHUNKS,)), dma((CHUNKS,)), dma(()), dma((2,)), dma((2,)), dma((2,)),
        ],
        compiler_params=pltpu.CompilerParams(
            collective_id=0, has_side_effects=True, vmem_limit_bytes=63 * 1024 * 1024
        ),
        cost_estimate=pl.CostEstimate(flops=10**9, bytes_accessed=4 * 10**6, transcendentals=700000),
    )(queries, key_states, value_states, past_keys, past_values, out_weight)
    return (own + other.astype(jnp.float32)).astype(bf16).T


def solution(mesh):
    placed = (
        P("ctx", "head"),
        P("ctx", "head"),
        P("ctx", "head"),
        P(None, "head"),
        P(None, "head"),
        P("head", None),
    )
    return jax.shard_map(
        body, mesh=mesh, in_specs=placed, out_specs=P("ctx", "head"), check_vma=False
    )
```

```python
import jax
import jax.numpy as jnp
from jax import lax
from jax.experimental import pallas as pl
from jax.experimental.pallas import tpu as pltpu
from jax.sharding import PartitionSpec as P

HEAD_DIM = 128
QUERY_SCALAR = 168
LOG2E = 1.4426950408889634
NZ = 8
NY = 8
BLK = 256
HALF = 128
CHUNKS = 4
CHUNK = BLK // CHUNKS
KEYS = 5 * BLK
SPAN = 1024 + HALF
COLS = 336
TILES = 21
MAIN = 640
TAIL = 32
ROWS = 16
MESH = pl.DeviceIdType.MESH
DIST = (0, 1, -1, 2, -2, 3, -3, 4)
SLOT = {d: i for i, d in enumerate(DIST)}


def kernel(
    q_hbm, k_hbm, v_hbm, pk_hbm, pv_hbm, w_hbm, own_hbm, other_hbm,
    q, kv, wrow, wsrc, wstage, wfull, att, acc, acc_t, xsend,
    z_ready, next_ready, in_sem, past_sem, own_sem, kv_send, kv_recv, fwd_send,
    w1_send, w1_recv, wy_send, wy_recv, ws_send, ws_recv,
    z1_send, z_send, z_recv, z4_recv, zs_send, zs_recv, x_send, x_recv,
):
    c = lax.axis_index("ctx")
    h = lax.axis_index("head")
    n_ctx = lax.axis_size("ctx")
    core = lax.rem(c, 2)
    c0 = c - core
    y = c // 4
    z = h // 2
    x_lo = lax.rem(h, 2)
    sibling = (c + 1 - 2 * core, h)
    partner = (c, h + 1 - 2 * x_lo)

    def at_z(d, of_core):
        return (c0 + of_core, lax.rem(z + d + NZ, NZ) * 2 + x_lo)

    def at_c(d):
        return (lax.rem(c + d + n_ctx, n_ctx), h)

    barrier = pltpu.get_barrier_semaphore()

    def greet(devices):
        for device in devices:
            pl.semaphore_signal(barrier, inc=1, device_id=device, device_id_type=MESH)

    def on_core(which):
        return pl.when(core == which)

    my_w = pl.ds(pl.multiple_of(y * 32 + core * ROWS, ROWS), ROWS)
    loads = [
        pltpu.make_async_copy(w_hbm.at[my_w], wrow, in_sem.at[0]),
        pltpu.make_async_copy(k_hbm, kv.at[0, pl.ds(4 * BLK, BLK)], in_sem.at[1]),
        pltpu.make_async_copy(v_hbm, kv.at[1, pl.ds(4 * BLK, BLK)], in_sem.at[2]),
        pltpu.make_async_copy(q_hbm, q, in_sem.at[3]),
    ]
    greet([sibling, partner, at_c(-2), at_c(-4)])

    def cores_at(t):
        return [(c0 + of_core, t * 2 + x_lo) for of_core in range(2)]

    @on_core(0)
    def _():
        @pl.when(z < NZ - 1)
        def _():
            greet(cores_at(z + 1)[:1])

        @pl.when(z == 0)
        def _():
            greet(cores_at(NZ - 1)[:1])

        for t in range(1, NZ):
            @pl.when(z < t)
            def _(t=t):
                greet(cores_at(t)[1:])

    @on_core(1)
    def _():
        greet([at_c(4)])
        for t in range(1, NZ):
            @pl.when(z < t)
            def _(t=t):
                greet(cores_at(t))

    for copy in loads:
        copy.start()

    def each_past(act):
        for first in range(4):
            @pl.when(c == first)
            def _(first=first):
                there = pl.ds(first * BLK, (4 - first) * BLK)
                here = pl.ds(0, (4 - first) * BLK)
                act(pltpu.make_async_copy(pk_hbm.at[there], kv.at[0, here], past_sem.at[0]))
                act(pltpu.make_async_copy(pv_hbm.at[there], kv.at[1, here], past_sem.at[1]))

    each_past(lambda copy: copy.start())

    with jax.named_scope("weight_rows"):
        loads[0].wait()
    group = lax.broadcasted_iota(jnp.int32, (ROWS, 128), 1) // TAIL
    for t in range(NZ):
        d = lax.rem(z - t + NZ, NZ)
        s = jnp.where(d > 4, 2 * (NZ - d), jnp.maximum(2 * d - 1, 0))
        at = t * 2 * COLS
        for i in range(5):
            wsrc[s, i] = wrow[:, at + i * 128 : at + (i + 1) * 128]
        tail = jnp.concatenate([wrow[:, at + MAIN : at + 2 * COLS]] * 4, axis=1)
        wsrc[s, 5] = jnp.where(group == lax.rem(s, 4), tail, jnp.zeros_like(tail))
    loads[1].wait()
    loads[2].wait()
    with jax.named_scope("entry"):
        neighbours = jnp.where(z >= 1, 1, 0) + jnp.where(z == NZ - 1, 1, 0)
        pl.semaphore_wait(barrier, jnp.where(core == 0, 4 + z + neighbours, 5 + 2 * z))

    def ready(sem, devices):
        for device in devices:
            pl.semaphore_signal(sem, inc=1, device_id=device, device_id_type=MESH)

    @on_core(0)
    def _():
        @pl.when(z >= 1)
        def _():
            ready(next_ready.at[0], cores_at(z - 1))

        @pl.when(z == NZ - 1)
        def _():
            ready(next_ready.at[1], cores_at(0))

    @on_core(1)
    def _():
        for t in range(NZ - 1):
            @pl.when(t < z)
            def _(t=t):
                ready(z_ready.at[z], cores_at(t))

    def remote(src, dst, send, recv, device):
        return pltpu.make_async_remote_copy(
            src_ref=src, dst_ref=dst, send_sem=send, recv_sem=recv, device_id=device, device_id_type=MESH
        )

    def all_of(ref, sem):
        return remote(ref, ref, sem, sem, sibling)

    def kv_slot(j):
        return kv.at[:, pl.ds(pl.multiple_of(j * BLK, BLK), BLK)]

    def kv_copy(j, device, send):
        return remote(kv_slot(4), kv_slot(j), send, kv_recv.at[j], device)

    def kv_start(j, device, send):
        for i in range(2):
            remote(kv_slot(4).at[i], kv_slot(j).at[i], send, kv_recv.at[j], device).start()

    to_far = kv_copy(0, at_c(4), kv_send.at[0])
    to_near = kv_copy(2, at_c(2), kv_send.at[1])
    to_next = kv_copy(3, sibling, kv_send.at[2])

    @pl.when(c + 2 < n_ctx)
    def _():
        kv_start(2, at_c(2), kv_send.at[1])

    @pl.when(c + 4 < n_ctx)
    def _():
        kv_start(0, at_c(4), kv_send.at[0])

    @on_core(0)
    def _():
        to_next.start()

    def w1_copy(s, of_core):
        return remote(wsrc.at[s], wstage.at[s, of_core], w1_send, w1_recv.at[s // 2], at_z(-DIST[s], 1))

    @on_core(0)
    def _():
        w1_copy(0, 0).start()

    def rounded_up(s):
        return DIST[s] if DIST[s] > 0 else NZ + DIST[s]

    def w1_below():
        for s in range(1, NZ):
            @pl.when(z >= rounded_up(s))
            def _(s=s):
                w1_copy(s, core).start()

    def w1_above(slots):
        for s in slots:
            @pl.when(z < rounded_up(s))
            def _(s=s):
                pl.semaphore_wait(z_ready.at[z + NZ - rounded_up(s)], 1)
                w1_copy(s, core).start()

    w1_below()

    near_slot = jnp.where(core == 0, 1, 3)
    fwd_near = remote(kv_slot(2), kv_slot(near_slot), fwd_send.at[0], kv_recv.at[near_slot], sibling)
    fwd_far = remote(kv_slot(0), kv_slot(1), fwd_send.at[1], kv_recv.at[1], sibling)

    def arrived(j):
        return remote(kv_slot(j), kv_slot(j), kv_send.at[0], kv_recv.at[j], sibling)

    def w_slab(n, dy):
        row = pl.multiple_of(lax.rem(y + dy + NY, NY) * 32, 32)
        tiles = pl.ds(10, 11) if n % 2 else pl.ds(0, 10)
        return wfull.at[n // 2, tiles, pl.ds(row, 32)]

    def wy_sem(n, way, step):
        return n * 7 + (step - 1) * 2 + (way + 1) // 2 if step < 4 else n * 7 + 6

    def wy_copy(n, way, step):
        slab = w_slab(n, -way * (step - 1))
        i = wy_sem(n, way, step)
        return remote(slab, slab, wy_send, wy_recv.at[i], at_c(4 * way))

    def wy_arrived(n, way, step):
        slab = w_slab(n, -way * step)
        i = wy_sem(n, way, step)
        return remote(slab, slab, wy_send, wy_recv.at[i], at_c(4 * way))

    def ws_copy(n, dy):
        slab = w_slab(n, dy)
        return remote(slab, slab, ws_send, ws_recv, sibling)

    def last_way(part):
        return 1 if part == 0 else -1

    def w_start(n):
        part = n // 2
        if n == 0:
            all_of(wsrc.at[pl.ds(0, 3)], w1_recv.at[0]).wait_recv()
        else:
            all_of(wstage.at[pl.ds(n * 2, 2)], w1_recv.at[n]).wait_recv()
        for of_core in range(2):
            rows = pl.ds(pl.multiple_of(y * 32 + of_core * ROWS, ROWS), ROWS)

            def piece(j, i):
                own = part * 4 + j == 0 and of_core == 1
                return wsrc[0, i] if own else wstage[part * 4 + j, of_core, i]

            for j in (n % 2 * 2, n % 2 * 2 + 1):
                for i in range(5):
                    wfull[part, j * 5 + i, rows] = piece(j, i)
            if n % 2:
                wfull[part, TILES - 1, rows] = piece(0, 5) + piece(1, 5) + piece(2, 5) + piece(3, 5)
        for way in (1, -1):
            wy_copy(n, way, 1).start()
        ws_copy(n, 0).start()

    def w_step(n, step):
        for way in (1, -1):
            if step == 4 and way != last_way(n % 2):
                continue
            wy_arrived(n, way, step).wait_recv()
            if step < 3 or (step == 3 and way == last_way(n % 2)):
                wy_copy(n, way, step + 1).start()
            ws_copy(n, 4 if step == 4 else -way * step).start()

    def weights(*todo):
        @on_core(1)
        def _():
            for n, step in todo:
                with jax.named_scope("weight_%d_hop_%d" % (n, step)):
                    w_step(n, step) if step else w_start(n)

    def far_block():
        with jax.named_scope("far_block"):
            @pl.when(c >= 4)
            def _():
                arrived(0).wait_recv()

        @pl.when((c >= 4) & (core == 1))
        def _():
            fwd_far.start()

    def near_block():
        with jax.named_scope("near_block"):
            @pl.when(c >= 2)
            def _():
                arrived(2).wait_recv()
                fwd_near.start()

    near_first = (core == 0) | (lax.rem(c // 2, 2) == 1)
    pl.when(z < NZ - 1)(lambda: weights((0, 0)))
    pl.when(near_first)(near_block)
    pl.when(jnp.logical_not(near_first))(far_block)
    w1_above((2, 4, 6))
    pl.when(near_first)(far_block)
    pl.when(jnp.logical_not(near_first))(near_block)
    pl.when(z >= 2)(lambda: w1_above((7, 5)))
    each_past(lambda copy: copy.wait())
    loads[3].wait()

    with jax.named_scope("passed_blocks"):
        @pl.when((c >= 1) | (core == 1))
        def _():
            arrived(3).wait_recv()

        @pl.when(c >= 3)
        def _():
            arrived(1).wait_recv()

    factor = QUERY_SCALAR ** (-0.5) * LOG2E
    row = lax.rem(lax.broadcasted_iota(jnp.int32, (2 * HALF, HALF), 0), HALF)
    col = lax.broadcasted_iota(jnp.int32, (2 * HALF, HALF), 1)

    def attend(half):
        rows = pl.ds(half * HALF, HALF)
        keys = kv[0, half * HALF : half * HALF + SPAN]
        values = kv[1, half * HALF : half * HALF + SPAN]
        both = jnp.concatenate([q[rows, :HEAD_DIM], q[rows, HEAD_DIM:]], axis=0)
        s = lax.dot_general(both, keys, (((1,), (1,)), ((), ())), preferred_element_type=jnp.float32)
        s = jnp.concatenate(
            [
                jnp.where(col > row, s[:, :HALF], -jnp.inf),
                s[:, HALF : SPAN - HALF],
                jnp.where(col <= row, s[:, SPAN - HALF :], -jnp.inf),
            ],
            axis=1,
        )
        m = jnp.max(s, axis=1, keepdims=True)
        p = jnp.exp2((s - m) * factor)
        total = jnp.sum(p, axis=1, keepdims=True)
        mixed = jnp.dot(p.astype(jnp.bfloat16), values, preferred_element_type=jnp.float32)
        mixed = (mixed * (1.0 / total)).astype(jnp.bfloat16)
        att[core, 0, rows, :HEAD_DIM] = mixed[:HALF]
        att[core, 0, rows, HEAD_DIM:] = mixed[HALF:]

    def rows_of(half):
        return pl.ds(half * HALF, HALF)

    def chunk_of(n):
        return pl.ds(n * CHUNK, CHUNK)

    def z_sem(n, way, step):
        return (n * 3 + step - 1) * 2 + (way + 1) // 2

    def z1_copy(n, way, of_core):
        rows = chunk_of(n)
        return remote(
            att.at[of_core, 0, rows], att.at[of_core, SLOT[-way], rows],
            z1_send, z_recv.at[z_sem(n, way, 1)], at_z(way, 0),
        )

    def z_copy(n, way, step):
        rows = chunk_of(n)
        return remote(
            att.at[:, SLOT[-way * (step - 1)], rows], att.at[:, SLOT[-way * step], rows],
            z_send, z_recv.at[z_sem(n, way, step)], at_z(way, 0),
        )

    def z4_copy(n, of_core):
        way = last_way(n % 2)
        rows = chunk_of(n)
        return remote(
            att.at[of_core, SLOT[-way * 3], rows], att.at[of_core, SLOT[4], rows],
            z_send, z4_recv.at[n], at_z(way, of_core),
        )

    def zs_copy(n, slot):
        rows = chunk_of(n)
        return remote(att.at[1, slot, rows], att.at[1, slot, rows], zs_send, zs_recv.at[n * 2 // CHUNKS], sibling)

    def z_step(n, step):
        for way in (-1, 1):
            here = att.at[:, SLOT[-way * step], chunk_of(n)]
            all_of(here, z_recv.at[z_sem(n, way, step)]).wait_recv()
            if step < 3:
                z_copy(n, way, step + 1).start()
            elif way == last_way(n % 2):
                for of_core in range(2):
                    z4_copy(n, of_core).start()
            zs_copy(n, SLOT[-way * step]).start()

    for half in range(2):
        with jax.named_scope("attend_%d" % half):
            attend(half)
        if half == 0:
            with jax.named_scope("next_ready"):
                @pl.when(z < NZ - 1)
                def _():
                    pl.semaphore_wait(next_ready.at[0], 1)

                @pl.when(z == 0)
                def _():
                    pl.semaphore_wait(next_ready.at[1], 1)
        for n in range(half * CHUNKS // 2, (half + 1) * CHUNKS // 2):
            for way in (1, -1):
                z1_copy(n, way, core).start()
    with jax.named_scope("weight_rows_up"):
        pl.when(z < 2)(lambda: w1_above((7, 5, 3, 1)))

    @on_core(0)
    def _():
        for step in range(1, 4):
            for n in range(CHUNKS):
                with jax.named_scope("attended_%d_hop_%d" % (n, step)):
                    z_step(n, step)
        with jax.named_scope("weights_from_core_1"):
            all_of(wfull, ws_recv).wait_recv()

    pl.when(z == 0)(lambda: weights((2, 0), (3, 0), (1, 0), *[(n, step) for step in range(1, 5) for n in (0, 2, 3, 1)]))

    @pl.when(z > 0)
    def _():
        pl.when(z == NZ - 1)(lambda: weights((0, 0)))
        weights((1, 0), (2, 0), (3, 0), *[(n, step) for step in range(1, 5) for n in range(4)])


    tail_of = lax.broadcasted_iota(jnp.int32, (HALF, 128), 1) // TAIL

    def project(half, slots):
        rows = rows_of(half)
        for s in slots:
            at = s % 4 * 5
            weight = jnp.concatenate(
                [wfull[s // 4, at + i] for i in range(5)] + [wfull[s // 4, TILES - 1]], axis=1
            )
            term = jnp.dot(att[core, s, rows, :], weight, preferred_element_type=jnp.float32)
            tail = jnp.where(tail_of == s % 4, term[:, MAIN:], 0.0)
            if s == 0:
                acc[rows, :MAIN] = term[:, :MAIN]
                acc[rows, MAIN:] = tail
            else:
                acc[rows, :MAIN] += term[:, :MAIN]
                acc[rows, MAIN:] += tail

    def x_copy(half):
        return remote(
            xsend.at[half], other_hbm.at[:, pl.ds(half * HALF, HALF)], x_send.at[half], x_recv.at[half], partner
        )

    def own_copy(half):
        mine = pl.ds(pl.multiple_of(x_lo * COLS, 16), COLS)
        return pltpu.make_async_copy(acc_t.at[half, mine], own_hbm.at[:, pl.ds(half * HALF, HALF)], own_sem.at[half])

    for half in range(2):
        rows = rows_of(half)
        with jax.named_scope("attended_from_core_0"):
            @on_core(1)
            def _(half=half):
                all_of(att.at[1, pl.ds(1, 6), rows_of(half)], zs_recv.at[half]).wait_recv()
        with jax.named_scope("project_%d" % half):
            project(half, range(7))
        with jax.named_scope("attended_%d_hop_4" % half):
            for n in range(half * CHUNKS // 2, (half + 1) * CHUNKS // 2):
                z4_copy(n, core).wait_recv()
        project(half, range(7, 8))
        tail = acc[rows, MAIN:].T
        acc_t[half, :MAIN] = acc[rows, :MAIN].T
        acc_t[half, MAIN:] = tail[:32] + tail[32:64] + tail[64:96] + tail[96:]
        theirs = pl.ds(pl.multiple_of((1 - x_lo) * COLS, 16), COLS)
        xsend[half] = acc_t[half, theirs].astype(jnp.bfloat16)
        x_copy(half).start()
        own_copy(half).start()

    with jax.named_scope("sent"):
        @pl.when(c + 2 < n_ctx)
        def _():
            to_near.wait_send()

        @pl.when(c + 4 < n_ctx)
        def _():
            to_far.wait_send()

        @pl.when(c >= 2)
        def _():
            fwd_near.wait_send()

        @pl.when((c >= 4) & (core == 1))
        def _():
            fwd_far.wait_send()

        all_of(att.at[0, pl.ds(0, 2)], z1_send).wait_send()

        @on_core(0)
        def _():
            to_next.wait_send()
            all_of(wsrc, w1_send).wait_send()
            all_of(att.at[:, pl.ds(0, 5)], z_send).wait_send()
            all_of(att.at[1, pl.ds(0, 6)], zs_send).wait_send()

        @on_core(1)
        def _():
            all_of(wsrc.at[pl.ds(0, 7)], w1_send).wait_send()
            all_of(wfull.at[:, :, pl.ds(0, 7 * 32)], wy_send).wait_send()
            all_of(wfull, ws_send).wait_send()

    with jax.named_scope("partner_sums"):
        for half in range(2):
            own_copy(half).wait()
            x_copy(half).wait()


def body(queries, key_states, value_states, past_keys, past_values, out_weight):
    bf16 = jnp.bfloat16
    dma = pltpu.SemaphoreType.DMA
    own, other = pl.pallas_call(
        kernel,
        out_shape=(jax.ShapeDtypeStruct((COLS, BLK), jnp.float32), jax.ShapeDtypeStruct((COLS, BLK), bf16)),
        in_specs=[pl.BlockSpec(memory_space=pl.ANY)] * 6,
        out_specs=(pl.BlockSpec(memory_space=pl.ANY),) * 2,
        scratch_shapes=[
            pltpu.VMEM((BLK, 2 * HEAD_DIM), bf16),
            pltpu.VMEM((2, KEYS, HEAD_DIM), bf16),
            pltpu.VMEM((ROWS, out_weight.shape[1]), bf16),
            pltpu.VMEM((NZ, 6, ROWS, 128), bf16),
            pltpu.VMEM((NZ, 2, 6, ROWS, 128), bf16),
            pltpu.VMEM((2, TILES, BLK, 128), bf16),
            pltpu.VMEM((2, NZ, BLK, 2 * HEAD_DIM), bf16),
            pltpu.VMEM((BLK, MAIN + 128), jnp.float32),
            pltpu.VMEM((2, 2 * COLS, HALF), jnp.float32),
            pltpu.VMEM((2, COLS, HALF), bf16),
            pltpu.SemaphoreType.REGULAR((8,)), pltpu.SemaphoreType.REGULAR((2,)),
            dma((4,)), dma((2,)), dma((2,)), dma((3,)), dma((4,)), dma((2,)),
            dma(()), dma((4,)), dma(()), dma((28,)), dma(()), dma(()),
            dma(()), dma(()), dma((6 * CHUNKS,)), dma((CHUNKS,)), dma(()), dma((2,)), dma((2,)), dma((2,)),
        ],
        compiler_params=pltpu.CompilerParams(
            collective_id=0, has_side_effects=True, vmem_limit_bytes=63 * 1024 * 1024
        ),
        cost_estimate=pl.CostEstimate(flops=10**9, bytes_accessed=4 * 10**6, transcendentals=700000),
    )(queries, key_states, value_states, past_keys, past_values, out_weight)
    return (own + other.astype(jnp.float32)).astype(bf16).T


def solution(mesh):
    placed = (
        P("ctx", "head"),
        P("ctx", "head"),
        P("ctx", "head"),
        P(None, "head"),
        P(None, "head"),
        P("head", None),
    )
    return jax.shard_map(
        body, mesh=mesh, in_specs=placed, out_specs=P("ctx", "head"), check_vma=False
    )
```

```python
import jax
import jax.numpy as jnp
from jax import lax
from jax.experimental import pallas as pl
from jax.experimental.pallas import tpu as pltpu
from jax.sharding import PartitionSpec as P

HEAD_DIM = 128
QUERY_SCALAR = 168
LOG2E = 1.4426950408889634
NZ = 8
NY = 8
BLK = 256
HALF = 128
CHUNKS = 4
CHUNK = BLK // CHUNKS
KEYS = 5 * BLK
SPAN = 1024 + HALF
COLS = 336
TILES = 21
MAIN = 640
TAIL = 32
ROWS = 16
MESH = pl.DeviceIdType.MESH
DIST = (0, 1, -1, 2, -2, 3, -3, 4)
SLOT = {d: i for i, d in enumerate(DIST)}


def kernel(
    q_hbm, k_hbm, v_hbm, pk_hbm, pv_hbm, w_hbm, own_hbm, other_hbm,
    q, kv, wrow, wsrc, wstage, wfull, att, acc, acc_t, xsend,
    z_ready, next_ready, in_sem, past_sem, own_sem, kv_send, kv_recv, fwd_send,
    w1_send, w1_recv, wy_send, wy_recv, ws_send, ws_recv,
    z1_send, z_send, z_recv, z4_recv, zs_send, zs_recv, x_send, x_recv,
):
    c = lax.axis_index("ctx")
    h = lax.axis_index("head")
    n_ctx = lax.axis_size("ctx")
    core = lax.rem(c, 2)
    c0 = c - core
    y = c // 4
    z = h // 2
    x_lo = lax.rem(h, 2)
    sibling = (c + 1 - 2 * core, h)
    partner = (c, h + 1 - 2 * x_lo)

    def at_z(d, of_core):
        return (c0 + of_core, lax.rem(z + d + NZ, NZ) * 2 + x_lo)

    def at_c(d):
        return (lax.rem(c + d + n_ctx, n_ctx), h)

    barrier = pltpu.get_barrier_semaphore()

    def greet(devices):
        for device in devices:
            pl.semaphore_signal(barrier, inc=1, device_id=device, device_id_type=MESH)

    def on_core(which):
        return pl.when(core == which)

    my_w = pl.ds(pl.multiple_of(y * 32 + core * ROWS, ROWS), ROWS)
    loads = [
        pltpu.make_async_copy(w_hbm.at[my_w], wrow, in_sem.at[0]),
        pltpu.make_async_copy(k_hbm, kv.at[0, pl.ds(4 * BLK, BLK)], in_sem.at[1]),
        pltpu.make_async_copy(v_hbm, kv.at[1, pl.ds(4 * BLK, BLK)], in_sem.at[2]),
        pltpu.make_async_copy(q_hbm, q, in_sem.at[3]),
    ]
    greet([sibling, partner, at_c(-2), at_c(-4)])

    def cores_at(t):
        return [(c0 + of_core, t * 2 + x_lo) for of_core in range(2)]

    @on_core(0)
    def _():
        @pl.when(z < NZ - 1)
        def _():
            greet(cores_at(z + 1)[:1])

        @pl.when(z == 0)
        def _():
            greet(cores_at(NZ - 1)[:1])

        for t in range(1, NZ):
            @pl.when(z < t)
            def _(t=t):
                greet(cores_at(t)[1:])

    @on_core(1)
    def _():
        greet([at_c(4)])
        for t in range(1, NZ):
            @pl.when(z < t)
            def _(t=t):
                greet(cores_at(t))

    for copy in loads:
        copy.start()

    def each_past(act):
        for first in range(4):
            @pl.when(c == first)
            def _(first=first):
                there = pl.ds(first * BLK, (4 - first) * BLK)
                here = pl.ds(0, (4 - first) * BLK)
                act(pltpu.make_async_copy(pk_hbm.at[there], kv.at[0, here], past_sem.at[0]))
                act(pltpu.make_async_copy(pv_hbm.at[there], kv.at[1, here], past_sem.at[1]))

    each_past(lambda copy: copy.start())

    with jax.named_scope("weight_rows"):
        loads[0].wait()
    group = lax.broadcasted_iota(jnp.int32, (ROWS, 128), 1) // TAIL
    for t in range(NZ):
        d = lax.rem(z - t + NZ, NZ)
        s = jnp.where(d > 4, 2 * (NZ - d), jnp.maximum(2 * d - 1, 0))
        at = t * 2 * COLS
        for i in range(5):
            wsrc[s, i] = wrow[:, at + i * 128 : at + (i + 1) * 128]
        tail = jnp.concatenate([wrow[:, at + MAIN : at + 2 * COLS]] * 4, axis=1)
        wsrc[s, 5] = jnp.where(group == lax.rem(s, 4), tail, jnp.zeros_like(tail))
    loads[1].wait()
    loads[2].wait()
    with jax.named_scope("entry"):
        neighbours = jnp.where(z >= 1, 1, 0) + jnp.where(z == NZ - 1, 1, 0)
        pl.semaphore_wait(barrier, jnp.where(core == 0, 4 + z + neighbours, 5 + 2 * z))

    def ready(sem, devices):
        for device in devices:
            pl.semaphore_signal(sem, inc=1, device_id=device, device_id_type=MESH)

    @on_core(0)
    def _():
        @pl.when(z >= 1)
        def _():
            ready(next_ready.at[0], cores_at(z - 1))

        @pl.when(z == NZ - 1)
        def _():
            ready(next_ready.at[1], cores_at(0))

    @on_core(1)
    def _():
        for t in range(NZ - 1):
            @pl.when(t < z)
            def _(t=t):
                ready(z_ready.at[z], cores_at(t))

    def remote(src, dst, send, recv, device):
        return pltpu.make_async_remote_copy(
            src_ref=src, dst_ref=dst, send_sem=send, recv_sem=recv, device_id=device, device_id_type=MESH
        )

    def all_of(ref, sem):
        return remote(ref, ref, sem, sem, sibling)

    def kv_slot(j):
        return kv.at[:, pl.ds(pl.multiple_of(j * BLK, BLK), BLK)]

    def kv_copy(j, device, send):
        return remote(kv_slot(4), kv_slot(j), send, kv_recv.at[j], device)

    def kv_start(j, device, send):
        for i in range(2):
            remote(kv_slot(4).at[i], kv_slot(j).at[i], send, kv_recv.at[j], device).start()

    to_far = kv_copy(0, at_c(4), kv_send.at[0])
    to_near = kv_copy(2, at_c(2), kv_send.at[1])
    to_next = kv_copy(3, sibling, kv_send.at[2])

    @pl.when(c + 2 < n_ctx)
    def _():
        kv_start(2, at_c(2), kv_send.at[1])

    @pl.when(c + 4 < n_ctx)
    def _():
        kv_start(0, at_c(4), kv_send.at[0])

    @on_core(0)
    def _():
        to_next.start()

    def w1_copy(s, of_core):
        return remote(wsrc.at[s], wstage.at[s, of_core], w1_send, w1_recv.at[s // 2], at_z(-DIST[s], 1))

    @on_core(0)
    def _():
        w1_copy(0, 0).start()

    def rounded_up(s):
        return DIST[s] if DIST[s] > 0 else NZ + DIST[s]

    def w1_below():
        for s in range(1, NZ):
            @pl.when(z >= rounded_up(s))
            def _(s=s):
                w1_copy(s, core).start()

    def w1_above(slots):
        for s in slots:
            @pl.when(z < rounded_up(s))
            def _(s=s):
                pl.semaphore_wait(z_ready.at[z + NZ - rounded_up(s)], 1)
                w1_copy(s, core).start()

    w1_below()

    near_slot = jnp.where(core == 0, 1, 3)
    fwd_near = remote(kv_slot(2), kv_slot(near_slot), fwd_send.at[0], kv_recv.at[near_slot], sibling)
    fwd_far = remote(kv_slot(0), kv_slot(1), fwd_send.at[1], kv_recv.at[1], sibling)

    def arrived(j):
        return remote(kv_slot(j), kv_slot(j), kv_send.at[0], kv_recv.at[j], sibling)

    def w_slab(n, dy):
        row = pl.multiple_of(lax.rem(y + dy + NY, NY) * 32, 32)
        tiles = pl.ds(10, 11) if n % 2 else pl.ds(0, 10)
        return wfull.at[n // 2, tiles, pl.ds(row, 32)]

    def wy_sem(n, way, step):
        return n * 7 + (step - 1) * 2 + (way + 1) // 2 if step < 4 else n * 7 + 6

    def wy_copy(n, way, step):
        slab = w_slab(n, -way * (step - 1))
        i = wy_sem(n, way, step)
        return remote(slab, slab, wy_send, wy_recv.at[i], at_c(4 * way))

    def wy_arrived(n, way, step):
        slab = w_slab(n, -way * step)
        i = wy_sem(n, way, step)
        return remote(slab, slab, wy_send, wy_recv.at[i], at_c(4 * way))

    def ws_copy(n, dy):
        slab = w_slab(n, dy)
        return remote(slab, slab, ws_send, ws_recv, sibling)

    def last_way(part):
        return 1 if part == 0 else -1

    def w_start(n):
        part = n // 2
        if n == 0:
            all_of(wsrc.at[pl.ds(0, 3)], w1_recv.at[0]).wait_recv()
        else:
            all_of(wstage.at[pl.ds(n * 2, 2)], w1_recv.at[n]).wait_recv()
        for of_core in range(2):
            rows = pl.ds(pl.multiple_of(y * 32 + of_core * ROWS, ROWS), ROWS)

            def piece(j, i):
                own = part * 4 + j == 0 and of_core == 1
                return wsrc[0, i] if own else wstage[part * 4 + j, of_core, i]

            for j in (n % 2 * 2, n % 2 * 2 + 1):
                for i in range(5):
                    wfull[part, j * 5 + i, rows] = piece(j, i)
            if n % 2:
                wfull[part, TILES - 1, rows] = piece(0, 5) + piece(1, 5) + piece(2, 5) + piece(3, 5)
        for way in (1, -1):
            wy_copy(n, way, 1).start()
        ws_copy(n, 0).start()

    def w_step(n, step):
        for way in (1, -1):
            if step == 4 and way != last_way(n % 2):
                continue
            wy_arrived(n, way, step).wait_recv()
            if step < 3 or (step == 3 and way == last_way(n % 2)):
                wy_copy(n, way, step + 1).start()
            ws_copy(n, 4 if step == 4 else -way * step).start()

    def weights(*todo):
        @on_core(1)
        def _():
            for n, step in todo:
                with jax.named_scope("weight_%d_hop_%d" % (n, step)):
                    w_step(n, step) if step else w_start(n)

    def far_block():
        with jax.named_scope("far_block"):
            @pl.when(c >= 4)
            def _():
                arrived(0).wait_recv()

        @pl.when((c >= 4) & (core == 1))
        def _():
            fwd_far.start()

    def near_block():
        with jax.named_scope("near_block"):
            @pl.when(c >= 2)
            def _():
                arrived(2).wait_recv()
                fwd_near.start()

    near_first = (core == 0) | (lax.rem(c // 2, 2) == 1)
    pl.when(z < NZ - 1)(lambda: weights((0, 0)))
    pl.when(near_first)(near_block)
    pl.when(jnp.logical_not(near_first))(far_block)
    w1_above((2, 4, 6))
    pl.when(near_first)(far_block)
    pl.when(jnp.logical_not(near_first))(near_block)
    pl.when(z >= 2)(lambda: w1_above((7, 5)))
    each_past(lambda copy: copy.wait())
    loads[3].wait()

    with jax.named_scope("passed_blocks"):
        @pl.when((c >= 1) | (core == 1))
        def _():
            arrived(3).wait_recv()

        @pl.when(c >= 3)
        def _():
            arrived(1).wait_recv()

    factor = QUERY_SCALAR ** (-0.5) * LOG2E
    row = lax.rem(lax.broadcasted_iota(jnp.int32, (2 * HALF, HALF), 0), HALF)
    col = lax.broadcasted_iota(jnp.int32, (2 * HALF, HALF), 1)

    def attend(half):
        rows = pl.ds(half * HALF, HALF)
        keys = kv[0, half * HALF : half * HALF + SPAN]
        values = kv[1, half * HALF : half * HALF + SPAN]
        both = jnp.concatenate([q[rows, :HEAD_DIM], q[rows, HEAD_DIM:]], axis=0)
        s = lax.dot_general(both, keys, (((1,), (1,)), ((), ())), preferred_element_type=jnp.float32)
        s = jnp.concatenate(
            [
                jnp.where(col > row, s[:, :HALF], -jnp.inf),
                s[:, HALF : SPAN - HALF],
                jnp.where(col <= row, s[:, SPAN - HALF :], -jnp.inf),
            ],
            axis=1,
        )
        m = jnp.max(s, axis=1, keepdims=True)
        p = jnp.exp2((s - m) * factor)
        total = jnp.sum(p, axis=1, keepdims=True)
        mixed = jnp.dot(p.astype(jnp.bfloat16), values, preferred_element_type=jnp.float32)
        mixed = (mixed * (1.0 / total)).astype(jnp.bfloat16)
        att[core, 0, rows, :HEAD_DIM] = mixed[:HALF]
        att[core, 0, rows, HEAD_DIM:] = mixed[HALF:]

    def rows_of(half):
        return pl.ds(half * HALF, HALF)

    def chunk_of(n):
        return pl.ds(n * CHUNK, CHUNK)

    def z_sem(n, way, step):
        return (n * 3 + step - 1) * 2 + (way + 1) // 2

    def z1_copy(n, way, of_core):
        rows = chunk_of(n)
        return remote(
            att.at[of_core, 0, rows], att.at[of_core, SLOT[-way], rows],
            z1_send, z_recv.at[z_sem(n, way, 1)], at_z(way, 0),
        )

    def z_copy(n, way, step):
        rows = chunk_of(n)
        return remote(
            att.at[:, SLOT[-way * (step - 1)], rows], att.at[:, SLOT[-way * step], rows],
            z_send, z_recv.at[z_sem(n, way, step)], at_z(way, 0),
        )

    def z4_copy(n, of_core):
        way = last_way(n % 2)
        rows = chunk_of(n)
        return remote(
            att.at[of_core, SLOT[-way * 3], rows], att.at[of_core, SLOT[4], rows],
            z_send, z4_recv.at[n], at_z(way, of_core),
        )

    def zs_copy(n, slot):
        rows = chunk_of(n)
        return remote(att.at[1, slot, rows], att.at[1, slot, rows], zs_send, zs_recv.at[n * 2 // CHUNKS], sibling)

    def z_step(n, step):
        for way in (-1, 1):
            here = att.at[:, SLOT[-way * step], chunk_of(n)]
            all_of(here, z_recv.at[z_sem(n, way, step)]).wait_recv()
            if step < 3:
                z_copy(n, way, step + 1).start()
            elif way == last_way(n % 2):
                for of_core in range(2):
                    z4_copy(n, of_core).start()
            zs_copy(n, SLOT[-way * step]).start()

    for half in range(2):
        with jax.named_scope("attend_%d" % half):
            attend(half)
        if half == 0:
            pl.when(z < 2)(lambda: w1_above((1, 3, 5, 7)))
            with jax.named_scope("next_ready"):
                @pl.when(z < NZ - 1)
                def _():
                    pl.semaphore_wait(next_ready.at[0], 1)

                @pl.when(z == 0)
                def _():
                    pl.semaphore_wait(next_ready.at[1], 1)
        for n in range(half * CHUNKS // 2, (half + 1) * CHUNKS // 2):
            for way in (1, -1):
                z1_copy(n, way, core).start()

    @on_core(0)
    def _():
        for step in range(1, 4):
            for n in range(CHUNKS):
                with jax.named_scope("attended_%d_hop_%d" % (n, step)):
                    z_step(n, step)
        with jax.named_scope("weights_from_core_1"):
            all_of(wfull, ws_recv).wait_recv()

    pl.when(z == 0)(lambda: weights((2, 0), (3, 0), (1, 0), *[(n, step) for step in range(1, 5) for n in (0, 2, 3, 1)]))

    @pl.when(z > 0)
    def _():
        pl.when(z == NZ - 1)(lambda: weights((0, 0)))
        weights((1, 0), (2, 0), (3, 0), *[(n, step) for step in range(1, 5) for n in range(4)])


    tail_of = lax.broadcasted_iota(jnp.int32, (HALF, 128), 1) // TAIL

    def project(half, slots):
        rows = rows_of(half)
        for s in slots:
            at = s % 4 * 5
            weight = jnp.concatenate(
                [wfull[s // 4, at + i] for i in range(5)] + [wfull[s // 4, TILES - 1]], axis=1
            )
            term = jnp.dot(att[core, s, rows, :], weight, preferred_element_type=jnp.float32)
            tail = jnp.where(tail_of == s % 4, term[:, MAIN:], 0.0)
            if s == 0:
                acc[rows, :MAIN] = term[:, :MAIN]
                acc[rows, MAIN:] = tail
            else:
                acc[rows, :MAIN] += term[:, :MAIN]
                acc[rows, MAIN:] += tail

    def x_copy(half):
        return remote(
            xsend.at[half], other_hbm.at[:, pl.ds(half * HALF, HALF)], x_send.at[half], x_recv.at[half], partner
        )

    def own_copy(half):
        mine = pl.ds(pl.multiple_of(x_lo * COLS, 16), COLS)
        return pltpu.make_async_copy(acc_t.at[half, mine], own_hbm.at[:, pl.ds(half * HALF, HALF)], own_sem.at[half])

    for half in range(2):
        rows = rows_of(half)
        with jax.named_scope("attended_from_core_0"):
            @on_core(1)
            def _(half=half):
                all_of(att.at[1, pl.ds(1, 6), rows_of(half)], zs_recv.at[half]).wait_recv()
        with jax.named_scope("project_%d" % half):
            project(half, range(7))
        with jax.named_scope("attended_%d_hop_4" % half):
            for n in range(half * CHUNKS // 2, (half + 1) * CHUNKS // 2):
                z4_copy(n, core).wait_recv()
        project(half, range(7, 8))
        tail = acc[rows, MAIN:].T
        acc_t[half, :MAIN] = acc[rows, :MAIN].T
        acc_t[half, MAIN:] = tail[:32] + tail[32:64] + tail[64:96] + tail[96:]
        theirs = pl.ds(pl.multiple_of((1 - x_lo) * COLS, 16), COLS)
        xsend[half] = acc_t[half, theirs].astype(jnp.bfloat16)
        x_copy(half).start()
        own_copy(half).start()

    with jax.named_scope("sent"):
        @pl.when(c + 2 < n_ctx)
        def _():
            to_near.wait_send()

        @pl.when(c + 4 < n_ctx)
        def _():
            to_far.wait_send()

        @pl.when(c >= 2)
        def _():
            fwd_near.wait_send()

        @pl.when((c >= 4) & (core == 1))
        def _():
            fwd_far.wait_send()

        all_of(att.at[0, pl.ds(0, 2)], z1_send).wait_send()

        @on_core(0)
        def _():
            to_next.wait_send()
            all_of(wsrc, w1_send).wait_send()
            all_of(att.at[:, pl.ds(0, 5)], z_send).wait_send()
            all_of(att.at[1, pl.ds(0, 6)], zs_send).wait_send()

        @on_core(1)
        def _():
            all_of(wsrc.at[pl.ds(0, 7)], w1_send).wait_send()
            all_of(wfull.at[:, :, pl.ds(0, 7 * 32)], wy_send).wait_send()
            all_of(wfull, ws_send).wait_send()

    with jax.named_scope("partner_sums"):
        for half in range(2):
            own_copy(half).wait()
            x_copy(half).wait()


def body(queries, key_states, value_states, past_keys, past_values, out_weight):
    bf16 = jnp.bfloat16
    dma = pltpu.SemaphoreType.DMA
    own, other = pl.pallas_call(
        kernel,
        out_shape=(jax.ShapeDtypeStruct((COLS, BLK), jnp.float32), jax.ShapeDtypeStruct((COLS, BLK), bf16)),
        in_specs=[pl.BlockSpec(memory_space=pl.ANY)] * 6,
        out_specs=(pl.BlockSpec(memory_space=pl.ANY),) * 2,
        scratch_shapes=[
            pltpu.VMEM((BLK, 2 * HEAD_DIM), bf16),
            pltpu.VMEM((2, KEYS, HEAD_DIM), bf16),
            pltpu.VMEM((ROWS, out_weight.shape[1]), bf16),
            pltpu.VMEM((NZ, 6, ROWS, 128), bf16),
            pltpu.VMEM((NZ, 2, 6, ROWS, 128), bf16),
            pltpu.VMEM((2, TILES, BLK, 128), bf16),
            pltpu.VMEM((2, NZ, BLK, 2 * HEAD_DIM), bf16),
            pltpu.VMEM((BLK, MAIN + 128), jnp.float32),
            pltpu.VMEM((2, 2 * COLS, HALF), jnp.float32),
            pltpu.VMEM((2, COLS, HALF), bf16),
            pltpu.SemaphoreType.REGULAR((8,)), pltpu.SemaphoreType.REGULAR((2,)),
            dma((4,)), dma((2,)), dma((2,)), dma((3,)), dma((4,)), dma((2,)),
            dma(()), dma((4,)), dma(()), dma((28,)), dma(()), dma(()),
            dma(()), dma(()), dma((6 * CHUNKS,)), dma((CHUNKS,)), dma(()), dma((2,)), dma((2,)), dma((2,)),
        ],
        compiler_params=pltpu.CompilerParams(
            collective_id=0, has_side_effects=True, vmem_limit_bytes=63 * 1024 * 1024
        ),
        cost_estimate=pl.CostEstimate(flops=10**9, bytes_accessed=4 * 10**6, transcendentals=700000),
    )(queries, key_states, value_states, past_keys, past_values, out_weight)
    return (own + other.astype(jnp.float32)).astype(bf16).T


def solution(mesh):
    placed = (
        P("ctx", "head"),
        P("ctx", "head"),
        P("ctx", "head"),
        P(None, "head"),
        P(None, "head"),
        P("head", None),
    )
    return jax.shard_map(
        body, mesh=mesh, in_specs=placed, out_specs=P("ctx", "head"), check_vma=False
    )
```

```python
import jax
import jax.numpy as jnp
from jax import lax
from jax.experimental import pallas as pl
from jax.experimental.pallas import tpu as pltpu
from jax.sharding import PartitionSpec as P

HEAD_DIM = 128
QUERY_SCALAR = 168
LOG2E = 1.4426950408889634
NZ = 8
NY = 8
BLK = 256
HALF = 128
CHUNKS = 4
CHUNK = BLK // CHUNKS
KEYS = 5 * BLK
SPAN = 1024 + HALF
COLS = 336
TILES = 21
MAIN = 640
TAIL = 32
ROWS = 16
MESH = pl.DeviceIdType.MESH
DIST = (0, 1, -1, 2, -2, 3, -3, 4)
SLOT = {d: i for i, d in enumerate(DIST)}


def kernel(
    q_hbm, k_hbm, v_hbm, pk_hbm, pv_hbm, w_hbm, own_hbm, other_hbm,
    q, kv, wrow, wsrc, wstage, wfull, att, acc, acc_t, xsend,
    z_ready, next_ready, in_sem, past_sem, own_sem, kv_send, kv_recv, fwd_send,
    w1_send, w1_recv, wy_send, wy_recv, ws_send, ws_recv,
    z1_send, z_send, z_recv, z4_recv, zs_send, zs_recv, x_send, x_recv,
):
    c = lax.axis_index("ctx")
    h = lax.axis_index("head")
    n_ctx = lax.axis_size("ctx")
    core = lax.rem(c, 2)
    c0 = c - core
    y = c // 4
    z = h // 2
    x_lo = lax.rem(h, 2)
    sibling = (c + 1 - 2 * core, h)
    partner = (c, h + 1 - 2 * x_lo)

    def at_z(d, of_core):
        return (c0 + of_core, lax.rem(z + d + NZ, NZ) * 2 + x_lo)

    def at_c(d):
        return (lax.rem(c + d + n_ctx, n_ctx), h)

    barrier = pltpu.get_barrier_semaphore()

    def greet(devices):
        for device in devices:
            pl.semaphore_signal(barrier, inc=1, device_id=device, device_id_type=MESH)

    def on_core(which):
        return pl.when(core == which)

    my_w = pl.ds(pl.multiple_of(y * 32 + core * ROWS, ROWS), ROWS)
    loads = [
        pltpu.make_async_copy(w_hbm.at[my_w], wrow, in_sem.at[0]),
        pltpu.make_async_copy(k_hbm, kv.at[0, pl.ds(4 * BLK, BLK)], in_sem.at[1]),
        pltpu.make_async_copy(v_hbm, kv.at[1, pl.ds(4 * BLK, BLK)], in_sem.at[2]),
        pltpu.make_async_copy(q_hbm, q, in_sem.at[3]),
    ]
    greet([sibling, partner, at_c(-2), at_c(-4)])

    def cores_at(t):
        return [(c0 + of_core, t * 2 + x_lo) for of_core in range(2)]

    @on_core(0)
    def _():
        @pl.when(z < NZ - 1)
        def _():
            greet(cores_at(z + 1)[:1])

        @pl.when(z == 0)
        def _():
            greet(cores_at(NZ - 1)[:1])

        for t in range(1, NZ):
            @pl.when(z < t)
            def _(t=t):
                greet(cores_at(t)[1:])

    @on_core(1)
    def _():
        greet([at_c(4)])
        for t in range(1, NZ):
            @pl.when(z < t)
            def _(t=t):
                greet(cores_at(t))

    for copy in loads:
        copy.start()

    def each_past(act):
        for first in range(4):
            @pl.when(c == first)
            def _(first=first):
                there = pl.ds(first * BLK, (4 - first) * BLK)
                here = pl.ds(0, (4 - first) * BLK)
                act(pltpu.make_async_copy(pk_hbm.at[there], kv.at[0, here], past_sem.at[0]))
                act(pltpu.make_async_copy(pv_hbm.at[there], kv.at[1, here], past_sem.at[1]))

    each_past(lambda copy: copy.start())

    with jax.named_scope("weight_rows"):
        loads[0].wait()
    group = lax.broadcasted_iota(jnp.int32, (ROWS, 128), 1) // TAIL
    for t in range(NZ):
        d = lax.rem(z - t + NZ, NZ)
        s = jnp.where(d > 4, 2 * (NZ - d), jnp.maximum(2 * d - 1, 0))
        at = t * 2 * COLS
        for i in range(5):
            wsrc[s, i] = wrow[:, at + i * 128 : at + (i + 1) * 128]
        tail = jnp.concatenate([wrow[:, at + MAIN : at + 2 * COLS]] * 4, axis=1)
        wsrc[s, 5] = jnp.where(group == lax.rem(s, 4), tail, jnp.zeros_like(tail))
    loads[1].wait()
    loads[2].wait()
    with jax.named_scope("entry"):
        neighbours = jnp.where(z >= 1, 1, 0) + jnp.where(z == NZ - 1, 1, 0)
        pl.semaphore_wait(barrier, jnp.where(core == 0, 4 + z + neighbours, 5 + 2 * z))

    def ready(sem, devices):
        for device in devices:
            pl.semaphore_signal(sem, inc=1, device_id=device, device_id_type=MESH)

    @on_core(0)
    def _():
        @pl.when(z >= 1)
        def _():
            ready(next_ready.at[0], cores_at(z - 1))

        @pl.when(z == NZ - 1)
        def _():
            ready(next_ready.at[1], cores_at(0))

    @on_core(1)
    def _():
        for t in range(NZ - 1):
            @pl.when(t < z)
            def _(t=t):
                ready(z_ready.at[z], cores_at(t))

    def remote(src, dst, send, recv, device):
        return pltpu.make_async_remote_copy(
            src_ref=src, dst_ref=dst, send_sem=send, recv_sem=recv, device_id=device, device_id_type=MESH
        )

    def all_of(ref, sem):
        return remote(ref, ref, sem, sem, sibling)

    def kv_slot(j):
        return kv.at[:, pl.ds(pl.multiple_of(j * BLK, BLK), BLK)]

    def kv_copy(j, device, send):
        return remote(kv_slot(4), kv_slot(j), send, kv_recv.at[j], device)

    def kv_start(j, device, send):
        for i in range(2):
            remote(kv_slot(4).at[i], kv_slot(j).at[i], send, kv_recv.at[j], device).start()

    to_far = kv_copy(0, at_c(4), kv_send.at[0])
    to_near = kv_copy(2, at_c(2), kv_send.at[1])
    to_next = kv_copy(3, sibling, kv_send.at[2])

    @pl.when(c + 2 < n_ctx)
    def _():
        kv_start(2, at_c(2), kv_send.at[1])

    @pl.when(c + 4 < n_ctx)
    def _():
        kv_start(0, at_c(4), kv_send.at[0])

    @on_core(0)
    def _():
        to_next.start()

    def w1_copy(s, of_core):
        return remote(wsrc.at[s], wstage.at[s, of_core], w1_send, w1_recv.at[s // 2], at_z(-DIST[s], 1))

    @on_core(0)
    def _():
        w1_copy(0, 0).start()

    def rounded_up(s):
        return DIST[s] if DIST[s] > 0 else NZ + DIST[s]

    def w1_below():
        for s in range(1, NZ):
            @pl.when(z >= rounded_up(s))
            def _(s=s):
                w1_copy(s, core).start()

    def w1_above(slots):
        for s in slots:
            @pl.when(z < rounded_up(s))
            def _(s=s):
                pl.semaphore_wait(z_ready.at[z + NZ - rounded_up(s)], 1)
                w1_copy(s, core).start()

    w1_below()

    near_slot = jnp.where(core == 0, 1, 3)
    fwd_near = remote(kv_slot(2), kv_slot(near_slot), fwd_send.at[0], kv_recv.at[near_slot], sibling)
    fwd_far = remote(kv_slot(0), kv_slot(1), fwd_send.at[1], kv_recv.at[1], sibling)

    def arrived(j):
        return remote(kv_slot(j), kv_slot(j), kv_send.at[0], kv_recv.at[j], sibling)

    def w_slab(n, dy):
        row = pl.multiple_of(lax.rem(y + dy + NY, NY) * 32, 32)
        tiles = pl.ds(10, 11) if n % 2 else pl.ds(0, 10)
        return wfull.at[n // 2, tiles, pl.ds(row, 32)]

    def wy_sem(n, way, step):
        return n * 7 + (step - 1) * 2 + (way + 1) // 2 if step < 4 else n * 7 + 6

    def wy_copy(n, way, step):
        slab = w_slab(n, -way * (step - 1))
        i = wy_sem(n, way, step)
        return remote(slab, slab, wy_send, wy_recv.at[i], at_c(4 * way))

    def wy_arrived(n, way, step):
        slab = w_slab(n, -way * step)
        i = wy_sem(n, way, step)
        return remote(slab, slab, wy_send, wy_recv.at[i], at_c(4 * way))

    def ws_copy(n, dy):
        slab = w_slab(n, dy)
        return remote(slab, slab, ws_send, ws_recv, sibling)

    def last_way(part):
        return 1 if part == 0 else -1

    def w_start(n):
        part = n // 2
        if n == 0:
            all_of(wsrc.at[pl.ds(0, 3)], w1_recv.at[0]).wait_recv()
        else:
            all_of(wstage.at[pl.ds(n * 2, 2)], w1_recv.at[n]).wait_recv()
        for of_core in range(2):
            rows = pl.ds(pl.multiple_of(y * 32 + of_core * ROWS, ROWS), ROWS)

            def piece(j, i):
                own = part * 4 + j == 0 and of_core == 1
                return wsrc[0, i] if own else wstage[part * 4 + j, of_core, i]

            for j in (n % 2 * 2, n % 2 * 2 + 1):
                for i in range(5):
                    wfull[part, j * 5 + i, rows] = piece(j, i)
            if n % 2:
                wfull[part, TILES - 1, rows] = piece(0, 5) + piece(1, 5) + piece(2, 5) + piece(3, 5)
        for way in (1, -1):
            wy_copy(n, way, 1).start()
        ws_copy(n, 0).start()

    def w_step(n, step):
        for way in (1, -1):
            if step == 4 and way != last_way(n % 2):
                continue
            wy_arrived(n, way, step).wait_recv()
            if step < 3 or (step == 3 and way == last_way(n % 2)):
                wy_copy(n, way, step + 1).start()
            ws_copy(n, 4 if step == 4 else -way * step).start()

    def weights(*todo):
        @on_core(1)
        def _():
            for n, step in todo:
                with jax.named_scope("weight_%d_hop_%d" % (n, step)):
                    w_step(n, step) if step else w_start(n)

    def far_block():
        with jax.named_scope("far_block"):
            @pl.when(c >= 4)
            def _():
                arrived(0).wait_recv()

        @pl.when((c >= 4) & (core == 1))
        def _():
            fwd_far.start()

    def near_block():
        with jax.named_scope("near_block"):
            @pl.when(c >= 2)
            def _():
                arrived(2).wait_recv()
                fwd_near.start()

    near_first = (core == 0) | (lax.rem(c // 2, 2) == 1)
    pl.when(z < NZ - 1)(lambda: weights((0, 0)))
    pl.when(near_first)(near_block)
    pl.when(jnp.logical_not(near_first))(far_block)
    w1_above((2, 4, 6))
    pl.when(near_first)(far_block)
    pl.when(jnp.logical_not(near_first))(near_block)
    pl.when(z >= 2)(lambda: w1_above((7, 5)))
    each_past(lambda copy: copy.wait())
    loads[3].wait()

    with jax.named_scope("passed_blocks"):
        @pl.when((c >= 1) | (core == 1))
        def _():
            arrived(3).wait_recv()

        @pl.when(c >= 3)
        def _():
            arrived(1).wait_recv()

    factor = QUERY_SCALAR ** (-0.5) * LOG2E
    row = lax.rem(lax.broadcasted_iota(jnp.int32, (2 * HALF, HALF), 0), HALF)
    col = lax.broadcasted_iota(jnp.int32, (2 * HALF, HALF), 1)

    def attend(half):
        rows = pl.ds(half * HALF, HALF)
        keys = kv[0, half * HALF : half * HALF + SPAN]
        values = kv[1, half * HALF : half * HALF + SPAN]
        both = jnp.concatenate([q[rows, :HEAD_DIM], q[rows, HEAD_DIM:]], axis=0)
        s = lax.dot_general(both, keys, (((1,), (1,)), ((), ())), preferred_element_type=jnp.float32)
        s = jnp.concatenate(
            [
                jnp.where(col > row, s[:, :HALF], -jnp.inf),
                s[:, HALF : SPAN - HALF],
                jnp.where(col <= row, s[:, SPAN - HALF :], -jnp.inf),
            ],
            axis=1,
        )
        m = jnp.max(s, axis=1, keepdims=True)
        p = jnp.exp2((s - m) * factor)
        total = jnp.sum(p, axis=1, keepdims=True)
        mixed = jnp.dot(p.astype(jnp.bfloat16), values, preferred_element_type=jnp.float32)
        mixed = (mixed * (1.0 / total)).astype(jnp.bfloat16)
        att[core, 0, rows, :HEAD_DIM] = mixed[:HALF]
        att[core, 0, rows, HEAD_DIM:] = mixed[HALF:]

    def rows_of(half):
        return pl.ds(half * HALF, HALF)

    def chunk_of(n):
        return pl.ds(n * CHUNK, CHUNK)

    def z_sem(n, way, step):
        return (n * 3 + step - 1) * 2 + (way + 1) // 2

    def z1_copy(n, way, of_core):
        rows = chunk_of(n)
        return remote(
            att.at[of_core, 0, rows], att.at[of_core, SLOT[-way], rows],
            z1_send, z_recv.at[z_sem(n, way, 1)], at_z(way, 0),
        )

    def z_copy(n, way, step):
        rows = chunk_of(n)
        return remote(
            att.at[:, SLOT[-way * (step - 1)], rows], att.at[:, SLOT[-way * step], rows],
            z_send, z_recv.at[z_sem(n, way, step)], at_z(way, 0),
        )

    def z4_copy(n, of_core):
        way = last_way(n % 2)
        rows = chunk_of(n)
        return remote(
            att.at[of_core, SLOT[-way * 3], rows], att.at[of_core, SLOT[4], rows],
            z_send, z4_recv.at[n], at_z(way, of_core),
        )

    def zs_copy(n, slot):
        rows = chunk_of(n)
        return remote(att.at[1, slot, rows], att.at[1, slot, rows], zs_send, zs_recv.at[n * 2 // CHUNKS], sibling)

    def z_step(n, step, ways):
        for way in ways:
            here = att.at[:, SLOT[-way * step], chunk_of(n)]
            all_of(here, z_recv.at[z_sem(n, way, step)]).wait_recv()
            if step < 3:
                z_copy(n, way, step + 1).start()
            elif way == last_way(n % 2):
                for of_core in range(2):
                    z4_copy(n, of_core).start()
            zs_copy(n, SLOT[-way * step]).start()

    for half in range(2):
        with jax.named_scope("attend_%d" % half):
            attend(half)
        if half == 0:
            pl.when(z < 2)(lambda: w1_above((1, 3, 5, 7)))
            with jax.named_scope("next_ready"):
                @pl.when(z < NZ - 1)
                def _():
                    pl.semaphore_wait(next_ready.at[0], 1)

                @pl.when(z == 0)
                def _():
                    pl.semaphore_wait(next_ready.at[1], 1)
        for n in range(half * CHUNKS // 2, (half + 1) * CHUNKS // 2):
            for way in (1, -1):
                z1_copy(n, way, core).start()

    def z_steps(ways):
        for step in range(1, 4):
            for n in range(CHUNKS):
                with jax.named_scope("attended_%d_hop_%d" % (n, step)):
                    z_step(n, step, ways)

    @on_core(0)
    def _():
        pl.when(z == 0)(lambda: z_steps((-1, 1)))
        pl.when(z > 0)(lambda: z_steps((1, -1)))
        with jax.named_scope("weights_from_core_1"):
            all_of(wfull, ws_recv).wait_recv()

    pl.when(z == 0)(lambda: weights((2, 0), (3, 0), (1, 0), *[(n, step) for step in range(1, 5) for n in (0, 2, 3, 1)]))

    @pl.when(z > 0)
    def _():
        pl.when(z == NZ - 1)(lambda: weights((0, 0)))
        weights((1, 0), (2, 0), (3, 0), *[(n, step) for step in range(1, 5) for n in range(4)])


    tail_of = lax.broadcasted_iota(jnp.int32, (HALF, 128), 1) // TAIL

    def project(half, slots):
        rows = rows_of(half)
        for s in slots:
            at = s % 4 * 5
            weight = jnp.concatenate(
                [wfull[s // 4, at + i] for i in range(5)] + [wfull[s // 4, TILES - 1]], axis=1
            )
            term = jnp.dot(att[core, s, rows, :], weight, preferred_element_type=jnp.float32)
            tail = jnp.where(tail_of == s % 4, term[:, MAIN:], 0.0)
            if s == 0:
                acc[rows, :MAIN] = term[:, :MAIN]
                acc[rows, MAIN:] = tail
            else:
                acc[rows, :MAIN] += term[:, :MAIN]
                acc[rows, MAIN:] += tail

    def x_copy(half):
        return remote(
            xsend.at[half], other_hbm.at[:, pl.ds(half * HALF, HALF)], x_send.at[half], x_recv.at[half], partner
        )

    def own_copy(half):
        mine = pl.ds(pl.multiple_of(x_lo * COLS, 16), COLS)
        return pltpu.make_async_copy(acc_t.at[half, mine], own_hbm.at[:, pl.ds(half * HALF, HALF)], own_sem.at[half])

    for half in range(2):
        rows = rows_of(half)
        with jax.named_scope("attended_from_core_0"):
            @on_core(1)
            def _(half=half):
                all_of(att.at[1, pl.ds(1, 6), rows_of(half)], zs_recv.at[half]).wait_recv()
        with jax.named_scope("project_%d" % half):
            project(half, range(7))
        with jax.named_scope("attended_%d_hop_4" % half):
            for n in range(half * CHUNKS // 2, (half + 1) * CHUNKS // 2):
                z4_copy(n, core).wait_recv()
        project(half, range(7, 8))
        tail = acc[rows, MAIN:].T
        acc_t[half, :MAIN] = acc[rows, :MAIN].T
        acc_t[half, MAIN:] = tail[:32] + tail[32:64] + tail[64:96] + tail[96:]
        theirs = pl.ds(pl.multiple_of((1 - x_lo) * COLS, 16), COLS)
        xsend[half] = acc_t[half, theirs].astype(jnp.bfloat16)
        x_copy(half).start()
        own_copy(half).start()

    with jax.named_scope("sent"):
        @pl.when(c + 2 < n_ctx)
        def _():
            to_near.wait_send()

        @pl.when(c + 4 < n_ctx)
        def _():
            to_far.wait_send()

        @pl.when(c >= 2)
        def _():
            fwd_near.wait_send()

        @pl.when((c >= 4) & (core == 1))
        def _():
            fwd_far.wait_send()

        all_of(att.at[0, pl.ds(0, 2)], z1_send).wait_send()

        @on_core(0)
        def _():
            to_next.wait_send()
            all_of(wsrc, w1_send).wait_send()
            all_of(att.at[:, pl.ds(0, 5)], z_send).wait_send()
            all_of(att.at[1, pl.ds(0, 6)], zs_send).wait_send()

        @on_core(1)
        def _():
            all_of(wsrc.at[pl.ds(0, 7)], w1_send).wait_send()
            all_of(wfull.at[:, :, pl.ds(0, 7 * 32)], wy_send).wait_send()
            all_of(wfull, ws_send).wait_send()

    with jax.named_scope("partner_sums"):
        for half in range(2):
            own_copy(half).wait()
            x_copy(half).wait()


def body(queries, key_states, value_states, past_keys, past_values, out_weight):
    bf16 = jnp.bfloat16
    dma = pltpu.SemaphoreType.DMA
    own, other = pl.pallas_call(
        kernel,
        out_shape=(jax.ShapeDtypeStruct((COLS, BLK), jnp.float32), jax.ShapeDtypeStruct((COLS, BLK), bf16)),
        in_specs=[pl.BlockSpec(memory_space=pl.ANY)] * 6,
        out_specs=(pl.BlockSpec(memory_space=pl.ANY),) * 2,
        scratch_shapes=[
            pltpu.VMEM((BLK, 2 * HEAD_DIM), bf16),
            pltpu.VMEM((2, KEYS, HEAD_DIM), bf16),
            pltpu.VMEM((ROWS, out_weight.shape[1]), bf16),
            pltpu.VMEM((NZ, 6, ROWS, 128), bf16),
            pltpu.VMEM((NZ, 2, 6, ROWS, 128), bf16),
            pltpu.VMEM((2, TILES, BLK, 128), bf16),
            pltpu.VMEM((2, NZ, BLK, 2 * HEAD_DIM), bf16),
            pltpu.VMEM((BLK, MAIN + 128), jnp.float32),
            pltpu.VMEM((2, 2 * COLS, HALF), jnp.float32),
            pltpu.VMEM((2, COLS, HALF), bf16),
            pltpu.SemaphoreType.REGULAR((8,)), pltpu.SemaphoreType.REGULAR((2,)),
            dma((4,)), dma((2,)), dma((2,)), dma((3,)), dma((4,)), dma((2,)),
            dma(()), dma((4,)), dma(()), dma((28,)), dma(()), dma(()),
            dma(()), dma(()), dma((6 * CHUNKS,)), dma((CHUNKS,)), dma(()), dma((2,)), dma((2,)), dma((2,)),
        ],
        compiler_params=pltpu.CompilerParams(
            collective_id=0, has_side_effects=True, vmem_limit_bytes=63 * 1024 * 1024
        ),
        cost_estimate=pl.CostEstimate(flops=10**9, bytes_accessed=4 * 10**6, transcendentals=700000),
    )(queries, key_states, value_states, past_keys, past_values, out_weight)
    return (own + other.astype(jnp.float32)).astype(bf16).T


def solution(mesh):
    placed = (
        P("ctx", "head"),
        P("ctx", "head"),
        P("ctx", "head"),
        P(None, "head"),
        P(None, "head"),
        P("head", None),
    )
    return jax.shard_map(
        body, mesh=mesh, in_specs=placed, out_specs=P("ctx", "head"), check_vma=False
    )
```
